1024 devices in a mesh: rep: 16 (over x, core), fsdp: 64 (over y, z).
Axes of the slice: x: 8, y: 8, z: 8, core: 2. Of those that a mesh axis runs over, the one named last changes fastest.
Arguments:
- partial_grads: bfloat16 [16, 192, 512, 512], P('rep', None, 'fsdp'), may hold values from -150 to 150
- block_owner: int32 [192], replicated, may hold values from 0 to 63, as said below
- block_slot: int32 [192], replicated, may hold values from 0 to 5, as said below
- left_roots: bfloat16 [384, 512, 512], P('fsdp'), may hold values from -1 to 2.5
- right_roots: bfloat16 [384, 512, 512], P('fsdp'), may hold values from -1 to 2.5
- momentum: float32 [192, 512, 512], P(None, 'fsdp', 'rep'), may hold values from -6 to 6
Outputs:
- new_momentum: float32 [192, 512, 512], P(None, 'fsdp', 'rep')
The draws below stay inside these ranges and needn't reach their ends.
Inputs may be any that keep to these rules, and one draw needn't show every extreme that they name: `block_owner`: every owner index names at least one block and at most 6 blocks; some index names exactly 6. `block_slot`: blocks with the same owner have different slots.
All inputs are finite; a program needn't handle non-finite values.
Results may differ from the reference program's by a relative error of at most 0.017.
Values may be sent and summed in bfloat16 or wider, within the bound.
No kernel may reach another device: no remote copies, remote signals or barrier semaphores. Data moves between devices by JAX's collectives and lax.ppermute only.
A program may use at most 64 MiB of HBM per device.

```python
import math
import jax
import jax.numpy as jnp
from jax import lax

BS = 512
MOST = 6
NB = 192
SLOTS = 384
N_REP = 16
N_FSDP = 64


def owner_entries(key):
    key_base, key_busy, key_pick, key_order = jax.random.split(key, 4)
    entry_count = N_FSDP * MOST
    base_scores = jax.random.permutation(key_base, entry_count).astype(jnp.int32)
    busiest = jax.random.randint(key_busy, (), 0, N_FSDP)
    chosen = jax.random.randint(key_pick, (N_FSDP,), 0, MOST)
    entries = jnp.arange(entry_count, dtype=jnp.int32)
    owner_index = entries // MOST
    slot_index = entries % MOST
    scores = base_scores - 2 * entry_count * (owner_index == busiest).astype(jnp.int32)
    scores = scores - entry_count * (slot_index == chosen[owner_index]).astype(jnp.int32)
    ordering = jnp.argsort(scores, stable=True)[:NB]
    shuffle = jax.random.permutation(key_order, NB)
    return ordering[shuffle].astype(jnp.int32)


def draw_block_owner(key, part):
    return (owner_entries(key) // MOST).astype(jnp.int32)


def draw_block_slot(key, part):
    return (owner_entries(key) % MOST).astype(jnp.int32)


def draw_partial_grads(key, part):
    key = jax.random.fold_in(key, 5)
    key_rows, key_cols, key_noise = jax.random.split(key, 3)
    shape = (N_REP, NB, BS, BS)
    row_scales = jnp.exp(jax.random.uniform(key_rows, (1, NB, BS, 1), jnp.float32, 0.0, math.log(10.0)))
    col_position = jnp.arange(BS, dtype=jnp.float32) / (BS - 1)
    rise_factor = 3.0
    noise_values = jax.random.truncated_normal(key_noise, -5.0, 5.0, shape, jnp.float32)
    overall = 0.05
    col_scales = jnp.exp(jax.random.uniform(key_cols, (1, NB, 1, BS), jnp.float32, 0.0, math.log(10.0)))
    col_scales = col_scales * jnp.power(rise_factor, 0.5 * col_position)
    return (overall * row_scales * col_scales * noise_values).astype(jnp.bfloat16)


def root_table(key, low, high, spread):
    key_diag, key_noise = jax.random.split(key)
    diagonal = jnp.exp(jax.random.uniform(key_diag, (SLOTS, BS, 1), jnp.float32, math.log(low), math.log(high)))
    noise_values = jax.random.truncated_normal(key_noise, -5.0, 5.0, (SLOTS, BS, BS), jnp.float32)
    symmetric = (noise_values + jnp.swapaxes(noise_values, 1, 2)) * (spread / math.sqrt(2.0 * BS))
    on_diagonal = jnp.arange(BS)[:, None] == jnp.arange(BS)[None, :]
    return jnp.where(on_diagonal[None, :, :], diagonal, symmetric).astype(jnp.bfloat16)


def draw_left_roots(key, part):
    key = jax.random.fold_in(key, 7)
    return root_table(key, 0.6, 1.4, 0.3)


def draw_right_roots(key, part):
    key = jax.random.fold_in(key, 9)
    return root_table(key, 0.6, 1.4, 0.3)


def block_levels(key, dims, pieces, low, largest):
    loudness = 1.0
    for position, blocks in pieces:
        steps = jax.random.uniform(jax.random.fold_in(jax.random.fold_in(key, 6), position), (blocks,), jnp.float32, low / len(pieces), largest / len(pieces))
        loudness = loudness * jnp.repeat(jnp.exp(steps), dims[position] // blocks).reshape((-1,) + (1,) * (len(dims) - 1 - position))
    return loudness


def gaussian(stream_key, dims, scale, limit, shards=(), kind=jnp.bfloat16):
    result = scale * jax.random.normal(stream_key, dims, jnp.float32)
    if shards:
        result = result * block_levels(stream_key, dims, shards, -0.22, 0.18)
    return jnp.clip(result, -limit, limit).astype(kind)


def setup_inputs(seed: int = 0) -> dict:
    splits = jax.random.split(jax.random.key(seed), 7)
    return {
        "partial_grads": draw_partial_grads(jax.random.fold_in(splits[6], 71), 0),
        "block_owner": draw_block_owner(jax.random.fold_in(splits[6], 71), 0),
        "block_slot": draw_block_slot(jax.random.fold_in(splits[6], 71), 0),
        "left_roots": draw_left_roots(jax.random.fold_in(splits[6], 71), 0),
        "right_roots": draw_right_roots(jax.random.fold_in(splits[6], 71), 0),
        "momentum": gaussian(splits[5], (NB, BS, BS), 1.0, 6.0, ((1, 64), (2, 16)), jnp.float32),
    }


def reference(partial_grads, block_owner, block_slot, left_roots, right_roots, momentum):

    def accumulate(running_sum, replica_part):
        return (running_sum + replica_part.astype(jnp.float32), None)
    summed, unused = lax.scan(accumulate, jnp.zeros(partial_grads.shape[1:], jnp.float32), partial_grads)
    grad = summed.astype(jnp.bfloat16)
    factor_row = (block_owner * MOST + block_slot).astype(jnp.int32)

    def precondition_block(block_args):
        grad_block, row_index = block_args
        left_root = left_roots[row_index]
        right_root = right_roots[row_index]
        right_prod = jnp.dot(grad_block, right_root, preferred_element_type=jnp.float32).astype(jnp.bfloat16)
        precond = jnp.dot(left_root, right_prod, preferred_element_type=jnp.float32)
        grad_float = grad_block.astype(jnp.float32)
        graft_scale = jnp.sqrt(jnp.mean(grad_float * grad_float)) / jnp.sqrt(jnp.mean(precond * precond) + 1e-06)
        return (precond * graft_scale).astype(jnp.bfloat16)
    grafted = lax.map(precondition_block, (grad, factor_row))
    return 0.9 * momentum + 0.1 * grafted.astype(jnp.float32)
```

```python
import functools

import jax
import jax.numpy as jnp
from jax import lax
from jax.experimental import pallas as pl
from jax.experimental.pallas import tpu as pltpu
from jax.sharding import Mesh, PartitionSpec as P

LANES = 128
VMEM = pl.BlockSpec(memory_space=pltpu.VMEM)
SMEM = pl.BlockSpec(memory_space=pltpu.SMEM)


def pair_sum_kernel(core_ref, place_ref, own_ref, other_ref, out_ref):
    del core_ref
    blocks = other_ref.shape[0]

    def body(b, carry):
        total = own_ref[b].astype(jnp.float32) + other_ref[b].astype(jnp.float32)
        out_ref[place_ref[b]] = total.astype(out_ref.dtype)
        return carry

    lax.fori_loop(0, blocks, body, 0, unroll=8)


def pair_sum(core, place, grads, other):
    blocks, rows, width = other.shape
    return pl.pallas_call(
        pair_sum_kernel,
        out_shape=jax.ShapeDtypeStruct(other.shape, other.dtype),
        grid_spec=pltpu.PrefetchScalarGridSpec(
            num_scalar_prefetch=2,
            grid=(1,),
            in_specs=[
                pl.BlockSpec((blocks, rows, width), lambda i, core, place: (core[0], 0, 0)),
                pl.BlockSpec((blocks, rows, width), lambda i, core, place: (0, 0, 0)),
            ],
            out_specs=pl.BlockSpec((blocks, rows, width), lambda i, core, place: (0, 0, 0)),
        ),
        compiler_params=pltpu.CompilerParams(vmem_limit_bytes=32 * 2**20),
        name="pair_sum",
    )(core, place, grads, other)


def sum_to_owner_kernel(owner_ref, parts_ref, out_ref):
    out_ref[...] = jnp.zeros_like(out_ref)
    for j in range(parts_ref.shape[1]):
        total = parts_ref[0, j].astype(jnp.float32)
        for i in range(1, parts_ref.shape[0]):
            total = total + parts_ref[i, j].astype(jnp.float32)
        out_ref[owner_ref[j]] = total.astype(out_ref.dtype)


def sum_to_owner(owner, parts, owner_count):
    return pl.pallas_call(
        sum_to_owner_kernel,
        out_shape=jax.ShapeDtypeStruct((owner_count,) + parts.shape[2:], parts.dtype),
        in_specs=[SMEM, VMEM],
        out_specs=VMEM,
        compiler_params=pltpu.CompilerParams(vmem_limit_bytes=32 * 2**20),
        name="sum_to_owner",
    )(owner, parts)


def precondition_kernel(slot_ref, grad_ref, left_ref, right_ref, out_ref):
    del slot_ref
    size = left_ref.shape[-1]
    grad = grad_ref[...].reshape(size, size)
    right_prod = jnp.dot(grad, right_ref[0], preferred_element_type=jnp.float32)
    precond = jnp.dot(
        left_ref[0], right_prod.astype(jnp.bfloat16), preferred_element_type=jnp.float32
    )
    grad_float = grad.astype(jnp.float32)
    area = float(size * size)
    grad_mean = jnp.sum(grad_float * grad_float, keepdims=True) / area
    precond_mean = jnp.sum(precond * precond, keepdims=True) / area
    scale = jnp.sqrt(grad_mean) / jnp.sqrt(precond_mean + 1e-06)
    out_ref[...] = (precond * scale).astype(out_ref.dtype).reshape(out_ref.shape)


def precondition(slot, grad, left_roots, right_roots):
    size = left_roots.shape[-1]
    whole = pl.BlockSpec(grad.shape, lambda i, slot: (0, 0, 0))
    factor = pl.BlockSpec((1, size, size), lambda i, slot: (slot[0], 0, 0))
    return pl.pallas_call(
        precondition_kernel,
        out_shape=jax.ShapeDtypeStruct(grad.shape, grad.dtype),
        grid_spec=pltpu.PrefetchScalarGridSpec(
            num_scalar_prefetch=1,
            grid=(1,),
            in_specs=[whole, factor, factor],
            out_specs=whole,
        ),
        compiler_params=pltpu.CompilerParams(vmem_limit_bytes=32 * 2**20),
        name="precondition",
    )(slot, grad, left_roots, right_roots)


def split_columns_kernel(owner_ref, rows_ref, out_ref):
    replicas, groups, rows, lanes = out_ref.shape
    width = rows_ref.shape[-1] // replicas
    per = lanes // width
    lane = lax.broadcasted_iota(jnp.int32, (rows, lanes), 1) // width
    for g in range(groups):
        blocks = [rows_ref[owner_ref[g * per + i]].astype(jnp.float32) for i in range(per)]
        for t in range(replicas // per):
            tiles = [block[:, t * lanes : (t + 1) * lanes] for block in blocks]
            for k in range(per):
                mixed = tiles[k]
                for i in range(per):
                    if i != k:
                        moved = pltpu.roll(tiles[i], ((i - k) % per) * width, 1)
                        mixed = jnp.where(lane == i, moved, mixed)
                out_ref[t * per + k, g] = mixed.astype(out_ref.dtype)


def split_columns(owner, rows, replicas):
    count = owner.shape[0]
    width = rows.shape[-1] // replicas
    per = LANES // width
    shape = (replicas, count // per, rows.shape[1], LANES)
    return pl.pallas_call(
        split_columns_kernel,
        out_shape=jax.ShapeDtypeStruct(shape, rows.dtype),
        in_specs=[SMEM, VMEM],
        out_specs=VMEM,
        compiler_params=pltpu.CompilerParams(vmem_limit_bytes=32 * 2**20),
        name="split_columns",
    )(owner, rows)


def update_kernel(place_ref, momentum_ref, pieces_ref, out_ref, block_ref):
    replicas, groups, _, lanes = pieces_ref.shape
    width = momentum_ref.shape[-1]
    per = lanes // width
    count = place_ref.shape[0]
    half = count // 2

    def invert(b, carry):
        block_ref[place_ref[b]] = b
        return carry

    lax.fori_loop(0, count, invert, 0, unroll=8)
    del half

    def body(r, carry):
        for g in range(groups):
            tile = pieces_ref[r, g].astype(jnp.float32)
            for i in range(per):
                piece = tile if i == 0 else pltpu.roll(tile, lanes - i * width, 1)
                b = block_ref[r * (groups * per) + g * per + i]
                out_ref[b] = 0.9 * momentum_ref[b] + 0.1 * piece[:, :width]
        return carry

    lax.fori_loop(0, replicas, body, 0, unroll=2)


def update(place, momentum, pieces):
    return pl.pallas_call(
        update_kernel,
        out_shape=jax.ShapeDtypeStruct(momentum.shape, momentum.dtype),
        in_specs=[SMEM, VMEM, VMEM],
        out_specs=VMEM,
        scratch_shapes=[pltpu.SMEM(place.shape, jnp.int32)],
        compiler_params=pltpu.CompilerParams(vmem_limit_bytes=32 * 2**20),
        name="update",
    )(place, momentum, pieces)


def on_device(partial_grads, block_owner, block_slot, left_roots, right_roots, momentum):
    owner_count = lax.axis_size("y") * lax.axis_size("z")
    planes = lax.axis_size("x")
    cores = lax.axis_size("core")
    replicas = planes * cores
    most = left_roots.shape[0]
    blocks, rows, width = partial_grads.shape[1:]
    half = blocks // cores
    each = half // planes
    core = lax.axis_index("core")
    plane = lax.axis_index("x")
    me = lax.axis_index(("y", "z"))
    grads = partial_grads[0]

    away = lax.dynamic_slice_in_dim(grads, (1 - core) * half, half, 0)
    other = lax.ppermute(away, "core", [(i, 1 - i) for i in range(cores)])

    owner = block_owner.reshape(cores, half)
    slot = block_slot.reshape(cores, half)
    entry = owner * most + slot
    rank = jnp.sum((entry[:, None, :] < entry[:, :, None]).astype(jnp.int32), axis=2)
    block_plane = rank % planes
    block_turn = rank // planes
    place = block_plane * each + block_turn
    own = lax.broadcasted_iota(jnp.int32, (cores, half), 0) == core
    mine = own & (block_plane == plane)
    turn_is = mine[None] & (
        block_turn[None] == lax.broadcasted_iota(jnp.int32, (each, cores, half), 0)
    )
    my_owner = jnp.sum(jnp.where(turn_is, owner[None], 0), axis=(1, 2))
    my_slot = jnp.sum(jnp.where(mine & (owner == me), slot, 0)).reshape(1)
    my_place = jnp.sum(jnp.where(own, place, 0), axis=0)
    piece_place = (
        (block_plane * cores + lax.broadcasted_iota(jnp.int32, (cores, half), 0)) * each
        + block_turn
    ).reshape(blocks)

    summed = pair_sum(core.reshape(1), my_place, grads, other)
    parts = lax.all_to_all(
        summed.reshape(planes, each, rows, width), "x", split_axis=0, concat_axis=0, tiled=True
    )
    to_owner = sum_to_owner(my_owner, parts, owner_count)
    grad = lax.all_to_all(to_owner, ("y", "z"), split_axis=0, concat_axis=0, tiled=True)
    grafted = precondition(my_slot, grad, left_roots, right_roots)
    back = lax.all_to_all(grafted, ("y", "z"), split_axis=0, concat_axis=0, tiled=True)
    pieces = split_columns(my_owner, back, replicas)
    pieces = lax.all_to_all(pieces, ("x", "core"), split_axis=0, concat_axis=0, tiled=True)
    return update(piece_place, momentum, pieces)


def solution(mesh):
    devices = mesh.devices.reshape(8, 2, 8, 8)
    split = Mesh(devices, ("x", "core", "y", "z"))
    rep, fsdp = ("x", "core"), ("y", "z")
    in_specs = (
        P(rep, None, fsdp, None),
        P(),
        P(),
        P(fsdp, None, None),
        P(fsdp, None, None),
        P(None, fsdp, rep),
    )
    out_specs = P(None, fsdp, rep)
    return jax.shard_map(
        on_device, mesh=split, in_specs=in_specs, out_specs=out_specs, check_vma=False
    )
```

```python
import functools

import jax
import jax.numpy as jnp
from jax import lax
from jax.experimental import pallas as pl
from jax.experimental.pallas import tpu as pltpu
from jax.sharding import Mesh, PartitionSpec as P

LANES = 128
VMEM = pl.BlockSpec(memory_space=pltpu.VMEM)
SMEM = pl.BlockSpec(memory_space=pltpu.SMEM)


def halves_kernel(core_ref, grads_ref, own_ref, away_ref, sems):
    width = own_ref.shape[2]
    copies = []
    for i, (side, out_ref) in enumerate(((core_ref[0], own_ref), (1 - core_ref[0], away_ref))):
        columns = pl.ds(pl.multiple_of(side * width, width), width)
        copies.append(pltpu.make_async_copy(grads_ref.at[:, :, columns], out_ref, sems.at[i]))
    for copy in copies:
        copy.start()
    for copy in copies:
        copy.wait()


def halves(core, grads):
    blocks, rows, width = grads.shape
    half = jax.ShapeDtypeStruct((blocks, rows, width // 2), grads.dtype)
    return pl.pallas_call(
        halves_kernel,
        out_shape=(half, half),
        in_specs=[SMEM, pl.BlockSpec(memory_space=pltpu.HBM)],
        out_specs=(VMEM, VMEM),
        scratch_shapes=[pltpu.SemaphoreType.DMA((2,))],
        compiler_params=pltpu.CompilerParams(vmem_limit_bytes=32 * 2**20),
        name="halves",
    )(core, grads)


def pair_sum_kernel(place_ref, own_ref, other_ref, out_ref):
    def body(b, carry):
        total = own_ref[b].astype(jnp.float32) + other_ref[b].astype(jnp.float32)
        out_ref[place_ref[b]] = total.astype(out_ref.dtype)
        return carry

    lax.fori_loop(0, own_ref.shape[0], body, 0, unroll=16)


def pair_sum(place, own, other):
    return pl.pallas_call(
        pair_sum_kernel,
        out_shape=jax.ShapeDtypeStruct(own.shape, own.dtype),
        in_specs=[SMEM, VMEM, VMEM],
        out_specs=VMEM,
        compiler_params=pltpu.CompilerParams(vmem_limit_bytes=32 * 2**20),
        name="pair_sum",
    )(place, own, other)


def sum_to_owner_kernel(owner_ref, parts_ref, out_ref):
    out_ref[...] = jnp.zeros_like(out_ref)
    for j in range(parts_ref.shape[1]):
        total = parts_ref[0, j].astype(jnp.float32)
        for i in range(1, parts_ref.shape[0]):
            total = total + parts_ref[i, j].astype(jnp.float32)
        out_ref[owner_ref[j]] = total.astype(out_ref.dtype)


def sum_to_owner(owner, parts, owner_count):
    return pl.pallas_call(
        sum_to_owner_kernel,
        out_shape=jax.ShapeDtypeStruct((owner_count,) + parts.shape[2:], parts.dtype),
        in_specs=[SMEM, VMEM],
        out_specs=VMEM,
        compiler_params=pltpu.CompilerParams(vmem_limit_bytes=32 * 2**20),
        name="sum_to_owner",
    )(owner, parts)


def precondition_kernel(core_ref, own_ref, other_ref, left_ref, right_ref, out_ref, *, slice_cols):
    size = left_ref.shape[-1]
    half = own_ref.shape[-1]
    cores = size // half
    area = float(size * size)
    core = core_ref[0]
    right_prod = jnp.zeros((size, size), jnp.float32)
    grad_squares = jnp.zeros((1, 1), jnp.float32)
    for side, grad_ref in ((core, own_ref), (1 - core, other_ref)):
        grad = grad_ref[...].reshape(size, half)
        factor = right_ref[pl.ds(pl.multiple_of(side * half, half), half), :]
        right_prod += jnp.dot(grad, factor, preferred_element_type=jnp.float32)
        grad_float = grad.astype(jnp.float32)
        grad_squares += jnp.sum(grad_float * grad_float, keepdims=True)
    precond = jnp.dot(
        left_ref[...], right_prod.astype(jnp.bfloat16), preferred_element_type=jnp.float32
    )
    precond_squares = jnp.sum(precond * precond, keepdims=True)
    scale = jnp.sqrt(grad_squares / area) / jnp.sqrt(precond_squares / area + 1e-06)
    grafted = (precond * scale).astype(jnp.bfloat16)
    column = lax.broadcasted_iota(jnp.int32, (size, half), 1)
    source = (column // slice_cols) * (slice_cols * cores) + core * slice_cols + column % slice_cols
    pick = (lax.broadcasted_iota(jnp.int32, (size, half), 0) == source).astype(jnp.bfloat16)
    picked = jnp.dot(grafted, pick, preferred_element_type=jnp.float32)
    out_ref[...] = picked.astype(out_ref.dtype).reshape(out_ref.shape)


def precondition(core, own, other, left_root, right_root, slice_cols):
    return pl.pallas_call(
        functools.partial(precondition_kernel, slice_cols=slice_cols),
        out_shape=jax.ShapeDtypeStruct(own.shape, own.dtype),
        in_specs=[SMEM, VMEM, VMEM, VMEM, VMEM],
        out_specs=VMEM,
        compiler_params=pltpu.CompilerParams(vmem_limit_bytes=32 * 2**20),
        name="precondition",
    )(core, own, other, left_root, right_root)


def split_columns_kernel(owner_ref, rows_ref, out_ref):
    replicas, groups, rows, lanes = out_ref.shape
    width = rows_ref.shape[-1] // replicas
    per = lanes // width
    lane = lax.broadcasted_iota(jnp.int32, (rows, lanes), 1) // width
    for g in range(groups):
        blocks = [rows_ref[owner_ref[g * per + i]].astype(jnp.float32) for i in range(per)]
        for t in range(replicas // per):
            tiles = [block[:, t * lanes : (t + 1) * lanes] for block in blocks]
            for k in range(per):
                mixed = tiles[k]
                for i in range(per):
                    if i != k:
                        moved = pltpu.roll(tiles[i], ((i - k) % per) * width, 1)
                        mixed = jnp.where(lane == i, moved, mixed)
                out_ref[t * per + k, g] = mixed.astype(out_ref.dtype)


def split_columns(owner, rows, replicas):
    count = owner.shape[0]
    width = rows.shape[-1] // replicas
    per = LANES // width
    shape = (replicas, count // per, rows.shape[1], LANES)
    return pl.pallas_call(
        split_columns_kernel,
        out_shape=jax.ShapeDtypeStruct(shape, rows.dtype),
        in_specs=[SMEM, VMEM],
        out_specs=VMEM,
        compiler_params=pltpu.CompilerParams(vmem_limit_bytes=32 * 2**20),
        name="split_columns",
    )(owner, rows)


def update_kernel(place_ref, momentum_ref, pieces_ref, out_ref, block_ref):
    replicas, groups, _, lanes = pieces_ref.shape
    width = momentum_ref.shape[-1]
    per = lanes // width
    count = place_ref.shape[0]

    def invert(b, carry):
        block_ref[place_ref[b]] = b
        return carry

    lax.fori_loop(0, count, invert, 0, unroll=8)
    def body(r, carry):
        for g in range(groups):
            tile = pieces_ref[r, g].astype(jnp.float32)
            for i in range(per):
                piece = tile if i == 0 else pltpu.roll(tile, lanes - i * width, 1)
                b = block_ref[r * (groups * per) + g * per + i]
                out_ref[b] = 0.9 * momentum_ref[b] + 0.1 * piece[:, :width]
        return carry

    lax.fori_loop(0, replicas, body, 0, unroll=2)


def update(place, momentum, pieces):
    return pl.pallas_call(
        update_kernel,
        out_shape=jax.ShapeDtypeStruct(momentum.shape, momentum.dtype),
        in_specs=[SMEM, VMEM, VMEM],
        out_specs=VMEM,
        scratch_shapes=[pltpu.SMEM(place.shape, jnp.int32)],
        compiler_params=pltpu.CompilerParams(vmem_limit_bytes=32 * 2**20),
        name="update",
    )(place, momentum, pieces)


def on_device(partial_grads, block_owner, block_slot, left_roots, right_roots, momentum):
    owner_count = lax.axis_size("y") * lax.axis_size("z")
    planes = lax.axis_size("x")
    cores = lax.axis_size("core")
    most = left_roots.shape[0]
    blocks, rows, width = partial_grads.shape[1:]
    each = blocks // planes
    half = width // cores
    core = lax.axis_index("core")
    plane = lax.axis_index("x")
    me = lax.axis_index(("y", "z"))

    swap = [(i, 1 - i) for i in range(cores)]
    grads = pltpu.with_memory_space_constraint(partial_grads[0], pltpu.HBM)
    own, away = halves(core.reshape(1), grads)
    other = lax.ppermute(away, "core", swap)

    entry = block_owner * most + block_slot
    rank = jnp.sum((entry[None, :] < entry[:, None]).astype(jnp.int32), axis=1)
    block_plane = rank % planes
    block_turn = rank // planes
    place = block_plane * each + block_turn
    mine = block_plane == plane
    turn_is = mine[None] & (
        block_turn[None] == lax.broadcasted_iota(jnp.int32, (each, blocks), 0)
    )
    my_owner = jnp.sum(jnp.where(turn_is, block_owner[None], 0), axis=1)
    my_slot = jnp.sum(jnp.where(mine & (block_owner == me), block_slot, 0))
    left_root = lax.dynamic_index_in_dim(left_roots, my_slot, 0, keepdims=False)
    right_root = lax.dynamic_index_in_dim(right_roots, my_slot, 0, keepdims=False)

    summed = pair_sum(place, own, other)
    parts = lax.all_to_all(
        summed.reshape(planes, each, rows, half), "x", split_axis=0, concat_axis=0, tiled=True
    )
    to_owner = sum_to_owner(my_owner, parts, owner_count)
    grad_half = lax.all_to_all(to_owner, ("y", "z"), split_axis=0, concat_axis=0, tiled=True)
    other_half = lax.ppermute(grad_half, "core", swap)
    grafted = precondition(
        core.reshape(1), grad_half, other_half, left_root, right_root, half // planes
    )
    back = lax.all_to_all(grafted, ("y", "z"), split_axis=0, concat_axis=0, tiled=True)
    pieces = split_columns(my_owner, back, planes)
    pieces = lax.all_to_all(pieces, "x", split_axis=0, concat_axis=0, tiled=True)
    return update(place, momentum, pieces)


def solution(mesh):
    devices = mesh.devices.reshape(8, 2, 8, 8)
    split = Mesh(devices, ("x", "core", "y", "z"))
    rep, fsdp = ("x", "core"), ("y", "z")
    in_specs = (
        P(rep, None, fsdp, None),
        P(),
        P(),
        P(fsdp, None, None),
        P(fsdp, None, None),
        P(None, fsdp, rep),
    )
    out_specs = P(None, fsdp, rep)
    return jax.shard_map(
        on_device, mesh=split, in_specs=in_specs, out_specs=out_specs, check_vma=False
    )
```

```python
import functools

import jax
import jax.numpy as jnp
from jax import lax
from jax.experimental import pallas as pl
from jax.experimental.pallas import tpu as pltpu
from jax.sharding import Mesh, PartitionSpec as P

LANES = 128
COPIES = 4
VMEM = pl.BlockSpec(memory_space=pltpu.VMEM)
SMEM = pl.BlockSpec(memory_space=pltpu.SMEM)


def column_copies(grads_ref, half_ref, sems, side):
    width = half_ref.shape[2]
    parts = sems.shape[0]
    count = half_ref.shape[0] // parts
    columns = pl.ds(pl.multiple_of(side * width, width), width)
    return [
        pltpu.make_async_copy(
            grads_ref.at[pl.ds(i * count, count), :, columns],
            half_ref.at[pl.ds(i * count, count)],
            sems.at[i],
        )
        for i in range(parts)
    ]


def away_half_kernel(core_ref, grads_ref, away_ref, sems):
    copies = column_copies(grads_ref, away_ref, sems, 1 - core_ref[0])
    for copy in copies:
        copy.start()
    for copy in copies:
        copy.wait()


def away_half(core, grads):
    blocks, rows, width = grads.shape
    return pl.pallas_call(
        away_half_kernel,
        out_shape=jax.ShapeDtypeStruct((blocks, rows, width // 2), grads.dtype),
        in_specs=[SMEM, pl.BlockSpec(memory_space=pltpu.HBM)],
        out_specs=VMEM,
        scratch_shapes=[pltpu.SemaphoreType.DMA((COPIES,))],
        compiler_params=pltpu.CompilerParams(vmem_limit_bytes=32 * 2**20),
        name="away_half",
    )(core, grads)


def pair_sum_kernel(core_ref, place_ref, grads_ref, other_ref, out_ref, own_ref, sems):
    copies = column_copies(grads_ref, own_ref, sems, core_ref[0])
    for copy in copies:
        copy.start()
    count = own_ref.shape[0] // len(copies)

    def body(b, carry):
        total = own_ref[b].astype(jnp.float32) + other_ref[b].astype(jnp.float32)
        out_ref[place_ref[b]] = total.astype(out_ref.dtype)
        return carry

    for i, copy in enumerate(copies):
        copy.wait()
        lax.fori_loop(i * count, (i + 1) * count, body, 0, unroll=16)


def pair_sum(core, place, grads, other):
    return pl.pallas_call(
        pair_sum_kernel,
        out_shape=jax.ShapeDtypeStruct(other.shape, other.dtype),
        in_specs=[SMEM, SMEM, pl.BlockSpec(memory_space=pltpu.HBM), VMEM],
        out_specs=VMEM,
        scratch_shapes=[
            pltpu.VMEM(other.shape, other.dtype),
            pltpu.SemaphoreType.DMA((COPIES,)),
        ],
        compiler_params=pltpu.CompilerParams(vmem_limit_bytes=32 * 2**20),
        name="pair_sum",
    )(core, place, grads, other)


def sum_to_owner_kernel(owner_ref, parts_ref, out_ref):
    out_ref[...] = jnp.zeros_like(out_ref)
    for j in range(parts_ref.shape[1]):
        total = parts_ref[0, j].astype(jnp.float32)
        for i in range(1, parts_ref.shape[0]):
            total = total + parts_ref[i, j].astype(jnp.float32)
        out_ref[owner_ref[j]] = total.astype(out_ref.dtype)


def sum_to_owner(owner, parts, owner_count):
    return pl.pallas_call(
        sum_to_owner_kernel,
        out_shape=jax.ShapeDtypeStruct((owner_count,) + parts.shape[2:], parts.dtype),
        in_specs=[SMEM, VMEM],
        out_specs=VMEM,
        compiler_params=pltpu.CompilerParams(vmem_limit_bytes=32 * 2**20),
        name="sum_to_owner",
    )(owner, parts)


def precondition_kernel(core_ref, own_ref, other_ref, left_ref, right_ref, out_ref, *, slice_cols):
    size = left_ref.shape[-1]
    half = own_ref.shape[-1]
    cores = size // half
    area = float(size * size)
    core = core_ref[0]
    right_prod = jnp.zeros((size, size), jnp.float32)
    grad_squares = jnp.zeros((1, 1), jnp.float32)
    for side, grad_ref in ((core, own_ref), (1 - core, other_ref)):
        grad = grad_ref[...].reshape(size, half)
        factor = right_ref[pl.ds(pl.multiple_of(side * half, half), half), :]
        right_prod += jnp.dot(grad, factor, preferred_element_type=jnp.float32)
        grad_float = grad.astype(jnp.float32)
        grad_squares += jnp.sum(grad_float * grad_float, keepdims=True)
    precond = jnp.dot(
        left_ref[...], right_prod.astype(jnp.bfloat16), preferred_element_type=jnp.float32
    )
    precond_squares = jnp.sum(precond * precond, keepdims=True)
    scale = jnp.sqrt(grad_squares / area) / jnp.sqrt(precond_squares / area + 1e-06)
    grafted = (precond * scale).astype(jnp.bfloat16)
    column = lax.broadcasted_iota(jnp.int32, (size, half), 1)
    source = (column // slice_cols) * (slice_cols * cores) + core * slice_cols + column % slice_cols
    pick = (lax.broadcasted_iota(jnp.int32, (size, half), 0) == source).astype(jnp.bfloat16)
    picked = jnp.dot(grafted, pick, preferred_element_type=jnp.float32)
    out_ref[...] = picked.astype(out_ref.dtype).reshape(out_ref.shape)


def precondition(core, own, other, left_root, right_root, slice_cols):
    return pl.pallas_call(
        functools.partial(precondition_kernel, slice_cols=slice_cols),
        out_shape=jax.ShapeDtypeStruct(own.shape, own.dtype),
        in_specs=[SMEM, VMEM, VMEM, VMEM, VMEM],
        out_specs=VMEM,
        compiler_params=pltpu.CompilerParams(vmem_limit_bytes=32 * 2**20),
        name="precondition",
    )(core, own, other, left_root, right_root)


def split_columns_kernel(owner_ref, rows_ref, out_ref):
    replicas, groups, rows, lanes = out_ref.shape
    width = rows_ref.shape[-1] // replicas
    per = lanes // width
    lane = lax.broadcasted_iota(jnp.int32, (rows, lanes), 1) // width
    for g in range(groups):
        blocks = [rows_ref[owner_ref[g * per + i]].astype(jnp.float32) for i in range(per)]
        for t in range(replicas // per):
            tiles = [block[:, t * lanes : (t + 1) * lanes] for block in blocks]
            for k in range(per):
                mixed = tiles[k]
                for i in range(per):
                    if i != k:
                        moved = pltpu.roll(tiles[i], ((i - k) % per) * width, 1)
                        mixed = jnp.where(lane == i, moved, mixed)
                out_ref[t * per + k, g] = mixed.astype(out_ref.dtype)


def split_columns(owner, rows, replicas):
    count = owner.shape[0]
    width = rows.shape[-1] // replicas
    per = LANES // width
    shape = (replicas, count // per, rows.shape[1], LANES)
    return pl.pallas_call(
        split_columns_kernel,
        out_shape=jax.ShapeDtypeStruct(shape, rows.dtype),
        in_specs=[SMEM, VMEM],
        out_specs=VMEM,
        compiler_params=pltpu.CompilerParams(vmem_limit_bytes=32 * 2**20),
        name="split_columns",
    )(owner, rows)


def update_kernel(place_ref, momentum_ref, pieces_ref, out_ref):
    replicas, groups, rows, lanes = pieces_ref.shape
    width, count = momentum_ref.shape[1:]
    per = lanes // width
    depth = replicas * groups * rows
    flipped = pieces_ref[...].astype(jnp.float32).reshape(depth, lanes).T.astype(jnp.bfloat16)
    place = place_ref[...]
    group = place // per
    turn = place % per
    source = lax.broadcasted_iota(jnp.int32, (depth, count), 0) - group * rows
    for row in range(rows):
        pick = (source == row).astype(jnp.bfloat16)
        spread = jnp.dot(flipped, pick, preferred_element_type=jnp.float32)
        value = jnp.zeros((width, count), jnp.float32)
        for i in range(per):
            value = jnp.where(turn == i, spread[i * width : (i + 1) * width], value)
        out_ref[row] = 0.9 * momentum_ref[row] + 0.1 * value


def update(place, momentum, pieces):
    flipped = pl.pallas_call(
        update_kernel,
        out_shape=jax.ShapeDtypeStruct(
            (momentum.shape[1], momentum.shape[2], momentum.shape[0]), momentum.dtype
        ),
        in_specs=[VMEM, VMEM, VMEM],
        out_specs=VMEM,
        compiler_params=pltpu.CompilerParams(vmem_limit_bytes=32 * 2**20),
        name="update",
    )(place.reshape(1, -1), jnp.transpose(momentum, (1, 2, 0)), pieces)
    return jnp.transpose(flipped, (2, 0, 1))


def on_device(partial_grads, block_owner, block_slot, left_roots, right_roots, momentum):
    owner_count = lax.axis_size("y") * lax.axis_size("z")
    planes = lax.axis_size("x")
    cores = lax.axis_size("core")
    most = left_roots.shape[0]
    blocks, rows, width = partial_grads.shape[1:]
    each = blocks // planes
    half = width // cores
    core = lax.axis_index("core")
    plane = lax.axis_index("x")
    me = lax.axis_index(("y", "z"))

    swap = [(i, 1 - i) for i in range(cores)]
    grads = pltpu.with_memory_space_constraint(partial_grads[0], pltpu.HBM)
    away = away_half(core.reshape(1), grads)
    other = lax.ppermute(away, "core", swap)

    entry = block_owner * most + block_slot
    rank = jnp.sum((entry[None, :] < entry[:, None]).astype(jnp.uint32), axis=1)
    place = (rank % planes * each + rank // planes).astype(jnp.int32)
    summed = pair_sum(core.reshape(1), place, grads, other)

    summed, rank, place = lax.optimization_barrier((summed, rank, place))
    parts = lax.all_to_all(
        summed.reshape(planes, each, rows, half), "x", split_axis=0, concat_axis=0, tiled=True
    )
    turns = lax.broadcasted_iota(jnp.uint32, (each, blocks), 0)
    turn_is = rank[None] == turns * planes + plane.astype(jnp.uint32)
    my_owner = jnp.sum(jnp.where(turn_is, block_owner[None], 0), axis=1)
    mine = (rank % planes == plane.astype(jnp.uint32)) & (block_owner == me)
    my_slot = jnp.sum(jnp.where(mine, block_slot, 0))
    left_root = lax.dynamic_index_in_dim(left_roots, my_slot, 0, keepdims=False)
    right_root = lax.dynamic_index_in_dim(right_roots, my_slot, 0, keepdims=False)
    parts, left_root, right_root = lax.optimization_barrier((parts, left_root, right_root))
    to_owner = sum_to_owner(my_owner, parts, owner_count)
    grad_half = lax.all_to_all(to_owner, ("y", "z"), split_axis=0, concat_axis=0, tiled=True)
    other_half = lax.ppermute(grad_half, "core", swap)
    grafted = precondition(
        core.reshape(1), grad_half, other_half, left_root, right_root, half // planes
    )
    back = lax.all_to_all(grafted, ("y", "z"), split_axis=0, concat_axis=0, tiled=True)
    pieces = split_columns(my_owner, back, planes)
    pieces = lax.all_to_all(pieces, "x", split_axis=0, concat_axis=0, tiled=True)
    return update(place, momentum, pieces)


def solution(mesh):
    devices = mesh.devices.reshape(8, 2, 8, 8)
    split = Mesh(devices, ("x", "core", "y", "z"))
    rep, fsdp = ("x", "core"), ("y", "z")
    in_specs = (
        P(rep, None, fsdp, None),
        P(),
        P(),
        P(fsdp, None, None),
        P(fsdp, None, None),
        P(None, fsdp, rep),
    )
    out_specs = P(None, fsdp, rep)
    return jax.shard_map(
        on_device, mesh=split, in_specs=in_specs, out_specs=out_specs, check_vma=False
    )
```

```python
import functools

import jax
import jax.numpy as jnp
from jax import lax
from jax.experimental import pallas as pl
from jax.experimental.pallas import tpu as pltpu
from jax.sharding import Mesh, PartitionSpec as P

LANES = 128
COPIES = 4
VMEM = pl.BlockSpec(memory_space=pltpu.VMEM)
SMEM = pl.BlockSpec(memory_space=pltpu.SMEM)


def column_half_kernel(side_ref, grads_ref, half_ref, sems):
    width = half_ref.shape[2]
    parts = sems.shape[0]
    count = half_ref.shape[0] // parts
    columns = pl.ds(pl.multiple_of(side_ref[0] * width, width), width)
    copies = [
        pltpu.make_async_copy(
            grads_ref.at[pl.ds(i * count, count), :, columns],
            half_ref.at[pl.ds(i * count, count)],
            sems.at[i],
        )
        for i in range(parts)
    ]
    for copy in copies:
        copy.start()
    for copy in copies:
        copy.wait()


def column_half(side, grads):
    blocks, rows, width = grads.shape
    return pl.pallas_call(
        column_half_kernel,
        out_shape=jax.ShapeDtypeStruct((blocks, rows, width // 2), grads.dtype),
        in_specs=[SMEM, pl.BlockSpec(memory_space=pltpu.HBM)],
        out_specs=VMEM,
        scratch_shapes=[pltpu.SemaphoreType.DMA((COPIES,))],
        compiler_params=pltpu.CompilerParams(vmem_limit_bytes=32 * 2**20),
        name="column_half",
    )(side.reshape(1), grads)


def pair_sum_kernel(place_ref, own_ref, other_ref, out_ref):
    for b in range(own_ref.shape[0]):
        out_ref[place_ref[b]] = own_ref[b] + other_ref[b]


def pair_sum(place, own, other):
    return pl.pallas_call(
        pair_sum_kernel,
        out_shape=jax.ShapeDtypeStruct(own.shape, own.dtype),
        in_specs=[SMEM, VMEM, VMEM],
        out_specs=VMEM,
        compiler_params=pltpu.CompilerParams(vmem_limit_bytes=32 * 2**20),
        name="pair_sum",
    )(place, own, other)


def sum_to_owner_kernel(owner_ref, parts_ref, out_ref):
    out_ref[...] = jnp.zeros_like(out_ref)
    for j in range(parts_ref.shape[1]):
        total = parts_ref[0, j].astype(jnp.float32)
        for i in range(1, parts_ref.shape[0]):
            total = total + parts_ref[i, j].astype(jnp.float32)
        out_ref[owner_ref[j]] = total.astype(out_ref.dtype)


def sum_to_owner(owner, parts, owner_count):
    return pl.pallas_call(
        sum_to_owner_kernel,
        out_shape=jax.ShapeDtypeStruct((owner_count,) + parts.shape[2:], parts.dtype),
        in_specs=[SMEM, VMEM],
        out_specs=VMEM,
        compiler_params=pltpu.CompilerParams(vmem_limit_bytes=32 * 2**20),
        name="sum_to_owner",
    )(owner, parts)


def fetch_roots_kernel(
    slot_ref, core_ref, left_table, right_table, left_ref, right_ref, raw_ref, sems, *, slice_cols
):
    slot = slot_ref[0]
    left_copy = pltpu.make_async_copy(left_table.at[slot], left_ref, sems.at[0])
    right_copy = pltpu.make_async_copy(right_table.at[slot], raw_ref, sems.at[1])
    right_copy.start()
    left_copy.start()
    size = raw_ref.shape[0]
    half = size // 2
    column = lax.broadcasted_iota(jnp.int32, (size, size), 1)
    inner = column % half
    side = jnp.where(column < half, core_ref[0], 1 - core_ref[0])
    source = inner // slice_cols * (2 * slice_cols) + side * slice_cols + inner % slice_cols
    pick = (lax.broadcasted_iota(jnp.int32, (size, size), 0) == source).astype(jnp.bfloat16)
    right_copy.wait()
    ordered = jnp.dot(raw_ref[...], pick, preferred_element_type=jnp.float32)
    right_ref[...] = ordered.astype(right_ref.dtype)
    left_copy.wait()


def fetch_roots(slot, core, left_roots, right_roots, slice_cols):
    root = jax.ShapeDtypeStruct(left_roots.shape[1:], left_roots.dtype)
    hbm = pl.BlockSpec(memory_space=pltpu.HBM)
    return pl.pallas_call(
        functools.partial(fetch_roots_kernel, slice_cols=slice_cols),
        out_shape=(root, root),
        in_specs=[SMEM, SMEM, hbm, hbm],
        out_specs=(VMEM, VMEM),
        scratch_shapes=[
            pltpu.VMEM(root.shape, root.dtype),
            pltpu.SemaphoreType.DMA((2,)),
        ],
        compiler_params=pltpu.CompilerParams(vmem_limit_bytes=32 * 2**20),
        name="fetch_roots",
    )(
        slot.reshape(1),
        core.reshape(1),
        pltpu.with_memory_space_constraint(left_roots, pltpu.HBM),
        pltpu.with_memory_space_constraint(right_roots, pltpu.HBM),
    )


def precondition_kernel(core_ref, own_ref, other_ref, left_ref, right_ref, out_ref):
    size = left_ref.shape[-1]
    half = own_ref.shape[-1]
    area = float(size * size)
    core = core_ref[0]
    right_prod = jnp.zeros((size, size), jnp.float32)
    grad_squares = jnp.zeros((1, 1), jnp.float32)
    for side, grad_ref in ((core, own_ref), (1 - core, other_ref)):
        grad = grad_ref[...].reshape(size, half)
        factor = right_ref[pl.ds(pl.multiple_of(side * half, half), half), :]
        right_prod += jnp.dot(grad, factor, preferred_element_type=jnp.float32)
        grad_float = grad.astype(jnp.float32)
        grad_squares += jnp.sum(grad_float * grad_float, keepdims=True)
    precond = jnp.dot(
        left_ref[...], right_prod.astype(jnp.bfloat16), preferred_element_type=jnp.float32
    )
    precond_squares = jnp.sum(precond * precond, keepdims=True)
    scale = jnp.sqrt(grad_squares / area) / jnp.sqrt(precond_squares / area + 1e-06)
    grafted = (precond[:, :half] * scale).astype(out_ref.dtype)
    out_ref[...] = grafted.reshape(out_ref.shape)


def precondition(core, own, other, left_root, right_root):
    return pl.pallas_call(
        precondition_kernel,
        out_shape=jax.ShapeDtypeStruct(own.shape, own.dtype),
        in_specs=[SMEM, VMEM, VMEM, VMEM, VMEM],
        out_specs=VMEM,
        compiler_params=pltpu.CompilerParams(vmem_limit_bytes=32 * 2**20),
        name="precondition",
    )(core.reshape(1), own, other, left_root, right_root)


def split_columns_kernel(owner_ref, rows_ref, out_ref):
    replicas, groups, rows, lanes = out_ref.shape
    width = rows_ref.shape[-1] // replicas
    per = lanes // width
    lane = lax.broadcasted_iota(jnp.int32, (rows, lanes), 1) // width
    for g in range(groups):
        blocks = [rows_ref[owner_ref[g * per + i]].astype(jnp.float32) for i in range(per)]
        for t in range(replicas // per):
            tiles = [block[:, t * lanes : (t + 1) * lanes] for block in blocks]
            for k in range(per):
                mixed = tiles[k]
                for i in range(per):
                    if i != k:
                        moved = pltpu.roll(tiles[i], ((i - k) % per) * width, 1)
                        mixed = jnp.where(lane == i, moved, mixed)
                out_ref[t * per + k, g] = mixed.astype(out_ref.dtype)


def split_columns(owner, rows, replicas):
    count = owner.shape[0]
    width = rows.shape[-1] // replicas
    per = LANES // width
    shape = (replicas, count // per, rows.shape[1], LANES)
    return pl.pallas_call(
        split_columns_kernel,
        out_shape=jax.ShapeDtypeStruct(shape, rows.dtype),
        in_specs=[SMEM, VMEM],
        out_specs=VMEM,
        compiler_params=pltpu.CompilerParams(vmem_limit_bytes=32 * 2**20),
        name="split_columns",
    )(owner, rows)


def update_kernel(place_ref, momentum_ref, pieces_ref, out_ref):
    replicas, groups, rows, lanes = pieces_ref.shape
    width, count = momentum_ref.shape[1:]
    per = lanes // width
    depth = replicas * groups * rows
    flipped = pieces_ref[...].astype(jnp.float32).reshape(depth, lanes).T.astype(jnp.bfloat16)
    place = place_ref[...]
    group = place // per
    turn = place % per
    source = lax.broadcasted_iota(jnp.int32, (depth, count), 0) - group * rows
    for row in range(rows):
        pick = (source == row).astype(jnp.bfloat16)
        spread = jnp.dot(flipped, pick, preferred_element_type=jnp.float32)
        value = jnp.zeros((width, count), jnp.float32)
        for i in range(per):
            value = jnp.where(turn == i, spread[i * width : (i + 1) * width], value)
        out_ref[row] = 0.9 * momentum_ref[row] + 0.1 * value


def update(place, momentum, pieces):
    flipped = pl.pallas_call(
        update_kernel,
        out_shape=jax.ShapeDtypeStruct(
            (momentum.shape[1], momentum.shape[2], momentum.shape[0]), momentum.dtype
        ),
        in_specs=[VMEM, VMEM, VMEM],
        out_specs=VMEM,
        compiler_params=pltpu.CompilerParams(vmem_limit_bytes=32 * 2**20),
        name="update",
    )(place.reshape(1, -1), jnp.transpose(momentum, (1, 2, 0)), pieces)
    return jnp.transpose(flipped, (2, 0, 1))


def on_device(partial_grads, block_owner, block_slot, left_roots, right_roots, momentum):
    owner_count = lax.axis_size("y") * lax.axis_size("z")
    planes = lax.axis_size("x")
    cores = lax.axis_size("core")
    most = left_roots.shape[0]
    blocks, rows, width = partial_grads.shape[1:]
    each = blocks // planes
    half = width // cores
    core = lax.axis_index("core")
    plane = lax.axis_index("x")
    me = lax.axis_index(("y", "z"))

    swap = [(i, 1 - i) for i in range(cores)]
    grads = pltpu.with_memory_space_constraint(partial_grads[0], pltpu.HBM)
    away = column_half(1 - core, grads)
    other = lax.ppermute(away, "core", swap)
    core_later, away = lax.optimization_barrier((core, away))
    own = column_half(core_later, grads)

    entry = block_owner * most + block_slot
    rank = jnp.sum((entry[None, :] < entry[:, None]).astype(jnp.uint32), axis=1)
    place = (rank % planes * each + rank // planes).astype(jnp.int32)
    summed = pair_sum(place, own, other)

    summed, rank, place = lax.optimization_barrier((summed, rank, place))
    parts = lax.all_to_all(
        summed.reshape(planes, each, rows, half), "x", split_axis=0, concat_axis=0, tiled=True
    )
    turns = lax.broadcasted_iota(jnp.uint32, (each, blocks), 0)
    turn_is = rank[None] == turns * planes + plane.astype(jnp.uint32)
    my_owner = jnp.sum(jnp.where(turn_is, block_owner[None], 0), axis=1)
    mine = (rank % planes == plane.astype(jnp.uint32)) & (block_owner == me)
    my_slot = jnp.sum(jnp.where(mine, block_slot, 0))
    left_root, right_root = fetch_roots(my_slot, core, left_roots, right_roots, half // planes)
    parts, left_root, right_root = lax.optimization_barrier((parts, left_root, right_root))
    to_owner = sum_to_owner(my_owner, parts, owner_count)
    grad_half = lax.all_to_all(to_owner, ("y", "z"), split_axis=0, concat_axis=0, tiled=True)
    other_half = lax.ppermute(grad_half, "core", swap)
    grafted = precondition(core, grad_half, other_half, left_root, right_root)
    back = lax.all_to_all(grafted, ("y", "z"), split_axis=0, concat_axis=0, tiled=True)
    pieces = split_columns(my_owner, back, planes)
    pieces = lax.all_to_all(pieces, "x", split_axis=0, concat_axis=0, tiled=True)
    return update(place, momentum, pieces)


def solution(mesh):
    devices = mesh.devices.reshape(8, 2, 8, 8)
    split = Mesh(devices, ("x", "core", "y", "z"))
    rep, fsdp = ("x", "core"), ("y", "z")
    in_specs = (
        P(rep, None, fsdp, None),
        P(),
        P(),
        P(fsdp, None, None),
        P(fsdp, None, None),
        P(None, fsdp, rep),
    )
    out_specs = P(None, fsdp, rep)
    return jax.shard_map(
        on_device, mesh=split, in_specs=in_specs, out_specs=out_specs, check_vma=False
    )
```

```python
import functools

import jax
import jax.numpy as jnp
from jax import lax
from jax.experimental import pallas as pl
from jax.experimental.pallas import tpu as pltpu
from jax.sharding import Mesh, PartitionSpec as P

LANES = 128
COPIES = 4
VMEM = pl.BlockSpec(memory_space=pltpu.VMEM)
SMEM = pl.BlockSpec(memory_space=pltpu.SMEM)


def column_half_kernel(side_ref, grads_ref, half_ref, sems):
    width = half_ref.shape[2]
    parts = sems.shape[0]
    count = half_ref.shape[0] // parts
    columns = pl.ds(pl.multiple_of(side_ref[0] * width, width), width)
    copies = [
        pltpu.make_async_copy(
            grads_ref.at[pl.ds(i * count, count), :, columns],
            half_ref.at[pl.ds(i * count, count)],
            sems.at[i],
        )
        for i in range(parts)
    ]
    for copy in copies:
        copy.start()
    for copy in copies:
        copy.wait()


def column_half(side, grads):
    blocks, rows, width = grads.shape
    return pl.pallas_call(
        column_half_kernel,
        out_shape=jax.ShapeDtypeStruct((blocks, rows, width // 2), grads.dtype),
        in_specs=[SMEM, pl.BlockSpec(memory_space=pltpu.HBM)],
        out_specs=VMEM,
        scratch_shapes=[pltpu.SemaphoreType.DMA((COPIES,))],
        compiler_params=pltpu.CompilerParams(vmem_limit_bytes=32 * 2**20),
        name="column_half",
    )(side.reshape(1), grads)


def pair_sum_kernel(block_ref, own_ref, other_ref, out_ref, sum_ref, sems):
    planes = sems.shape[0]
    each = own_ref.shape[0] // planes
    copies = []
    for plane in range(planes):
        for p in range(plane * each, (plane + 1) * each):
            b = block_ref[p]
            sum_ref[p] = own_ref[b] + other_ref[b]
        part = pl.ds(plane * each, each)
        copies.append(pltpu.make_async_copy(sum_ref.at[part], out_ref.at[part], sems.at[plane]))
        copies[-1].start()
    for copy in copies:
        copy.wait()


def pair_sum(block_at, own, other, planes):
    return pl.pallas_call(
        pair_sum_kernel,
        out_shape=jax.ShapeDtypeStruct(own.shape, own.dtype),
        in_specs=[SMEM, VMEM, VMEM],
        out_specs=pl.BlockSpec(memory_space=pltpu.HBM),
        scratch_shapes=[
            pltpu.VMEM(own.shape, own.dtype),
            pltpu.SemaphoreType.DMA((planes,)),
        ],
        compiler_params=pltpu.CompilerParams(vmem_limit_bytes=32 * 2**20),
        name="pair_sum",
    )(block_at, own, other)


def sum_to_owner_kernel(owner_ref, parts_ref, out_ref):
    out_ref[...] = jnp.zeros_like(out_ref)
    for j in range(parts_ref.shape[1]):
        total = parts_ref[0, j].astype(jnp.float32)
        for i in range(1, parts_ref.shape[0]):
            total = total + parts_ref[i, j].astype(jnp.float32)
        out_ref[owner_ref[j]] = total.astype(out_ref.dtype)


def sum_to_owner(owner, parts, owner_count):
    return pl.pallas_call(
        sum_to_owner_kernel,
        out_shape=jax.ShapeDtypeStruct((owner_count,) + parts.shape[2:], parts.dtype),
        in_specs=[SMEM, VMEM],
        out_specs=VMEM,
        compiler_params=pltpu.CompilerParams(vmem_limit_bytes=32 * 2**20),
        name="sum_to_owner",
    )(owner, parts)


def fetch_roots_kernel(
    slot_ref, core_ref, left_table, right_table, left_ref, right_ref, raw_ref, sems, *, slice_cols
):
    slot = slot_ref[0]
    left_copy = pltpu.make_async_copy(left_table.at[slot], left_ref, sems.at[0])
    right_copy = pltpu.make_async_copy(right_table.at[slot], raw_ref, sems.at[1])
    right_copy.start()
    left_copy.start()
    size = raw_ref.shape[0]
    half = size // 2
    column = lax.broadcasted_iota(jnp.int32, (size, size), 1)
    inner = column % half
    side = jnp.where(column < half, core_ref[0], 1 - core_ref[0])
    source = inner // slice_cols * (2 * slice_cols) + side * slice_cols + inner % slice_cols
    pick = (lax.broadcasted_iota(jnp.int32, (size, size), 0) == source).astype(jnp.bfloat16)
    right_copy.wait()
    ordered = jnp.dot(raw_ref[...], pick, preferred_element_type=jnp.float32)
    right_ref[...] = ordered.astype(right_ref.dtype)
    left_copy.wait()


def fetch_roots(slot, core, left_roots, right_roots, slice_cols):
    root = jax.ShapeDtypeStruct(left_roots.shape[1:], left_roots.dtype)
    hbm = pl.BlockSpec(memory_space=pltpu.HBM)
    return pl.pallas_call(
        functools.partial(fetch_roots_kernel, slice_cols=slice_cols),
        out_shape=(root, root),
        in_specs=[SMEM, SMEM, hbm, hbm],
        out_specs=(VMEM, VMEM),
        scratch_shapes=[
            pltpu.VMEM(root.shape, root.dtype),
            pltpu.SemaphoreType.DMA((2,)),
        ],
        compiler_params=pltpu.CompilerParams(vmem_limit_bytes=32 * 2**20),
        name="fetch_roots",
    )(
        slot.reshape(1),
        core.reshape(1),
        pltpu.with_memory_space_constraint(left_roots, pltpu.HBM),
        pltpu.with_memory_space_constraint(right_roots, pltpu.HBM),
    )


def half_product(core_ref, grad_ref, right_ref, opposite):
    size, half = right_ref.shape[0], grad_ref.shape[-1]
    side = 1 - core_ref[0] if opposite else core_ref[0]
    grad = grad_ref[...].reshape(size, half)
    factor = right_ref[pl.ds(pl.multiple_of(side * half, half), half), :]
    product = jnp.dot(grad, factor, preferred_element_type=jnp.float32)
    grad_float = grad.astype(jnp.float32)
    return product, jnp.sum(grad_float * grad_float, keepdims=True)


def own_product_kernel(core_ref, own_ref, right_ref, product_ref, squares_ref):
    product, squares = half_product(core_ref, own_ref, right_ref, False)
    product_ref[...] = product
    squares_ref[...] = jnp.broadcast_to(squares, squares_ref.shape)


def own_product(core, own, right_root):
    return pl.pallas_call(
        own_product_kernel,
        out_shape=(
            jax.ShapeDtypeStruct(right_root.shape, jnp.float32),
            jax.ShapeDtypeStruct((1, LANES), jnp.float32),
        ),
        in_specs=[SMEM, VMEM, VMEM],
        out_specs=(VMEM, VMEM),
        compiler_params=pltpu.CompilerParams(vmem_limit_bytes=32 * 2**20),
        name="own_product",
    )(core.reshape(1), own, right_root)


def precondition_kernel(
    core_ref, product_ref, squares_ref, other_ref, left_ref, right_ref, out_ref
):
    size = left_ref.shape[-1]
    half = other_ref.shape[-1]
    area = float(size * size)
    product, squares = half_product(core_ref, other_ref, right_ref, True)
    right_prod = (product_ref[...] + product).astype(jnp.bfloat16)
    grad_squares = squares_ref[:, :1] + squares
    precond = jnp.dot(left_ref[...], right_prod, preferred_element_type=jnp.float32)
    precond_squares = jnp.sum(precond * precond, keepdims=True)
    scale = jnp.sqrt(grad_squares / area) / jnp.sqrt(precond_squares / area + 1e-06)
    grafted = (precond[:, :half] * scale).astype(out_ref.dtype)
    out_ref[...] = grafted.reshape(out_ref.shape)


def precondition(core, product, squares, other, left_root, right_root):
    return pl.pallas_call(
        precondition_kernel,
        out_shape=jax.ShapeDtypeStruct(other.shape, other.dtype),
        in_specs=[SMEM, VMEM, VMEM, VMEM, VMEM, VMEM],
        out_specs=VMEM,
        compiler_params=pltpu.CompilerParams(vmem_limit_bytes=32 * 2**20),
        name="precondition",
    )(core.reshape(1), product, squares, other, left_root, right_root)


def split_columns_kernel(owner_ref, rows_ref, out_ref):
    replicas, groups, rows, lanes = out_ref.shape
    width = rows_ref.shape[-1] // replicas
    per = lanes // width
    lane = lax.broadcasted_iota(jnp.int32, (rows, lanes), 1) // width
    for g in range(groups):
        blocks = [rows_ref[owner_ref[g * per + i]].astype(jnp.float32) for i in range(per)]
        for t in range(replicas // per):
            tiles = [block[:, t * lanes : (t + 1) * lanes] for block in blocks]
            for k in range(per):
                mixed = tiles[k]
                for i in range(per):
                    if i != k:
                        moved = pltpu.roll(tiles[i], ((i - k) % per) * width, 1)
                        mixed = jnp.where(lane == i, moved, mixed)
                out_ref[t * per + k, g] = mixed.astype(out_ref.dtype)


def split_columns(owner, rows, replicas):
    count = owner.shape[0]
    width = rows.shape[-1] // replicas
    per = LANES // width
    shape = (replicas, count // per, rows.shape[1], LANES)
    return pl.pallas_call(
        split_columns_kernel,
        out_shape=jax.ShapeDtypeStruct(shape, rows.dtype),
        in_specs=[SMEM, VMEM],
        out_specs=VMEM,
        compiler_params=pltpu.CompilerParams(vmem_limit_bytes=32 * 2**20),
        name="split_columns",
    )(owner, rows)


def update_kernel(place_ref, momentum_ref, pieces_ref, out_ref):
    replicas, groups, rows, lanes = pieces_ref.shape
    width, count = momentum_ref.shape[1:]
    per = lanes // width
    depth = replicas * groups * rows
    flipped = pieces_ref[...].astype(jnp.float32).reshape(depth, lanes).T.astype(jnp.bfloat16)
    place = place_ref[...]
    group = place // per
    turn = place % per
    source = lax.broadcasted_iota(jnp.int32, (depth, count), 0) - group * rows
    for row in range(rows):
        pick = (source == row).astype(jnp.bfloat16)
        spread = jnp.dot(flipped, pick, preferred_element_type=jnp.float32)
        value = jnp.zeros((width, count), jnp.float32)
        for i in range(per):
            value = jnp.where(turn == i, spread[i * width : (i + 1) * width], value)
        out_ref[row] = 0.9 * momentum_ref[row] + 0.1 * value


def update(place, momentum, pieces):
    flipped = pl.pallas_call(
        update_kernel,
        out_shape=jax.ShapeDtypeStruct(
            (momentum.shape[1], momentum.shape[2], momentum.shape[0]), momentum.dtype
        ),
        in_specs=[VMEM, VMEM, VMEM],
        out_specs=VMEM,
        compiler_params=pltpu.CompilerParams(vmem_limit_bytes=32 * 2**20),
        name="update",
    )(place.reshape(1, -1), jnp.transpose(momentum, (1, 2, 0)), pieces)
    return jnp.transpose(flipped, (2, 0, 1))


def on_device(partial_grads, block_owner, block_slot, left_roots, right_roots, momentum):
    owner_count = lax.axis_size("y") * lax.axis_size("z")
    planes = lax.axis_size("x")
    cores = lax.axis_size("core")
    most = left_roots.shape[0]
    blocks, rows, width = partial_grads.shape[1:]
    each = blocks // planes
    half = width // cores
    core = lax.axis_index("core")
    plane = lax.axis_index("x")
    me = lax.axis_index(("y", "z"))

    swap = [(i, 1 - i) for i in range(cores)]
    grads = pltpu.with_memory_space_constraint(partial_grads[0], pltpu.HBM)
    away = column_half(1 - core, grads)
    other = lax.ppermute(away, "core", swap)
    core_later, away = lax.optimization_barrier((core, away))
    own = column_half(core_later, grads)

    entry = block_owner * most + block_slot
    rank = jnp.sum((entry[None, :] < entry[:, None]).astype(jnp.uint32), axis=1)
    place = (rank % planes * each + rank // planes).astype(jnp.int32)
    order = lax.iota(jnp.int32, blocks)
    block_at = jnp.sum(jnp.where(place[None, :] == order[:, None], order[None, :], 0), axis=1)
    summed = pair_sum(block_at, own, other, planes)

    summed, rank, place = lax.optimization_barrier((summed, rank, place))
    parts = lax.all_to_all(
        summed.reshape(planes, each, rows, half), "x", split_axis=0, concat_axis=0, tiled=True
    )
    turns = lax.broadcasted_iota(jnp.uint32, (each, blocks), 0)
    turn_is = rank[None] == turns * planes + plane.astype(jnp.uint32)
    my_owner = jnp.sum(jnp.where(turn_is, block_owner[None], 0), axis=1)
    mine = (rank % planes == plane.astype(jnp.uint32)) & (block_owner == me)
    my_slot = jnp.sum(jnp.where(mine, block_slot, 0))
    left_root, right_root = fetch_roots(my_slot, core, left_roots, right_roots, half // planes)
    parts, left_root, right_root = lax.optimization_barrier((parts, left_root, right_root))
    to_owner = sum_to_owner(my_owner, parts, owner_count)
    grad_half = lax.all_to_all(to_owner, ("y", "z"), split_axis=0, concat_axis=0, tiled=True)
    other_half = lax.ppermute(grad_half, "core", swap)
    product, squares = own_product(core, grad_half, right_root)
    grafted = precondition(core, product, squares, other_half, left_root, right_root)
    back = lax.all_to_all(grafted, ("y", "z"), split_axis=0, concat_axis=0, tiled=True)
    pieces = split_columns(my_owner, back, planes)
    pieces = lax.all_to_all(pieces, "x", split_axis=0, concat_axis=0, tiled=True)
    return update(place, momentum, pieces)


def solution(mesh):
    devices = mesh.devices.reshape(8, 2, 8, 8)
    split = Mesh(devices, ("x", "core", "y", "z"))
    rep, fsdp = ("x", "core"), ("y", "z")
    in_specs = (
        P(rep, None, fsdp, None),
        P(),
        P(),
        P(fsdp, None, None),
        P(fsdp, None, None),
        P(None, fsdp, rep),
    )
    out_specs = P(None, fsdp, rep)
    return jax.shard_map(
        on_device, mesh=split, in_specs=in_specs, out_specs=out_specs, check_vma=False
    )
```

```python
import functools

import jax
import jax.numpy as jnp
from jax import lax
from jax.experimental import pallas as pl
from jax.experimental.pallas import tpu as pltpu
from jax.sharding import Mesh, PartitionSpec as P

LANES = 128
COPIES = 4
VMEM = pl.BlockSpec(memory_space=pltpu.VMEM)
SMEM = pl.BlockSpec(memory_space=pltpu.SMEM)


def column_half_kernel(side_ref, grads_ref, half_ref, sems):
    width = half_ref.shape[2]
    parts = sems.shape[0]
    count = half_ref.shape[0] // parts
    columns = pl.ds(pl.multiple_of(side_ref[0] * width, width), width)
    copies = [
        pltpu.make_async_copy(
            grads_ref.at[pl.ds(i * count, count), :, columns],
            half_ref.at[pl.ds(i * count, count)],
            sems.at[i],
        )
        for i in range(parts)
    ]
    for copy in copies:
        copy.start()
    for copy in copies:
        copy.wait()


def column_half(side, grads):
    blocks, rows, width = grads.shape
    return pl.pallas_call(
        column_half_kernel,
        out_shape=jax.ShapeDtypeStruct((blocks, rows, width // 2), grads.dtype),
        in_specs=[SMEM, pl.BlockSpec(memory_space=pltpu.HBM)],
        out_specs=VMEM,
        scratch_shapes=[pltpu.SemaphoreType.DMA((COPIES,))],
        compiler_params=pltpu.CompilerParams(vmem_limit_bytes=32 * 2**20),
        name="column_half",
    )(side.reshape(1), grads)


def pair_sum_kernel(block_ref, own_ref, other_ref, keep_ref, away_ref):
    count = keep_ref.shape[0]
    for p in range(own_ref.shape[0]):
        b = block_ref[p]
        total = own_ref[b] + other_ref[b]
        if p < count:
            keep_ref[p] = total
        else:
            away_ref[p - count] = total


def pair_sum(block_at, own, other):
    part = jax.ShapeDtypeStruct((own.shape[0] // 2,) + own.shape[1:], own.dtype)
    return pl.pallas_call(
        pair_sum_kernel,
        out_shape=(part, part),
        in_specs=[SMEM, VMEM, VMEM],
        out_specs=(VMEM, VMEM),
        compiler_params=pltpu.CompilerParams(vmem_limit_bytes=32 * 2**20),
        name="pair_sum",
    )(block_at, own, other)


def sum_to_owner_kernel(owner_ref, parts_ref, out_ref):
    out_ref[...] = jnp.zeros_like(out_ref)
    for j in range(parts_ref.shape[1]):
        total = parts_ref[0, j].astype(jnp.float32)
        for i in range(1, parts_ref.shape[0]):
            total = total + parts_ref[i, j].astype(jnp.float32)
        out_ref[owner_ref[j]] = total.astype(out_ref.dtype)


def sum_to_owner(owner, parts, owner_count):
    return pl.pallas_call(
        sum_to_owner_kernel,
        out_shape=jax.ShapeDtypeStruct((owner_count,) + parts.shape[2:], parts.dtype),
        in_specs=[SMEM, VMEM],
        out_specs=VMEM,
        compiler_params=pltpu.CompilerParams(vmem_limit_bytes=32 * 2**20),
        name="sum_to_owner",
    )(owner, parts)


def fetch_roots_kernel(
    slot_ref, core_ref, left_table, right_table, left_ref, right_ref, raw_ref, sems, *, slice_cols
):
    slot = slot_ref[0]
    left_copy = pltpu.make_async_copy(left_table.at[slot], left_ref, sems.at[0])
    right_copy = pltpu.make_async_copy(right_table.at[slot], raw_ref, sems.at[1])
    right_copy.start()
    left_copy.start()
    size = raw_ref.shape[0]
    half = size // 2
    column = lax.broadcasted_iota(jnp.int32, (size, size), 1)
    inner = column % half
    side = jnp.where(column < half, core_ref[0], 1 - core_ref[0])
    source = inner // slice_cols * (2 * slice_cols) + side * slice_cols + inner % slice_cols
    pick = (lax.broadcasted_iota(jnp.int32, (size, size), 0) == source).astype(jnp.bfloat16)
    right_copy.wait()
    ordered = jnp.dot(raw_ref[...], pick, preferred_element_type=jnp.float32)
    right_ref[...] = ordered.astype(right_ref.dtype)
    left_copy.wait()


def fetch_roots(slot, core, left_roots, right_roots, slice_cols):
    root = jax.ShapeDtypeStruct(left_roots.shape[1:], left_roots.dtype)
    hbm = pl.BlockSpec(memory_space=pltpu.HBM)
    return pl.pallas_call(
        functools.partial(fetch_roots_kernel, slice_cols=slice_cols),
        out_shape=(root, root),
        in_specs=[SMEM, SMEM, hbm, hbm],
        out_specs=(VMEM, VMEM),
        scratch_shapes=[
            pltpu.VMEM(root.shape, root.dtype),
            pltpu.SemaphoreType.DMA((2,)),
        ],
        compiler_params=pltpu.CompilerParams(vmem_limit_bytes=32 * 2**20),
        name="fetch_roots",
    )(
        slot.reshape(1),
        core.reshape(1),
        pltpu.with_memory_space_constraint(left_roots, pltpu.HBM),
        pltpu.with_memory_space_constraint(right_roots, pltpu.HBM),
    )


def half_product(core_ref, grad_ref, right_ref, opposite):
    size, half = right_ref.shape[0], grad_ref.shape[-1]
    side = 1 - core_ref[0] if opposite else core_ref[0]
    grad = grad_ref[...].reshape(size, half)
    factor = right_ref[pl.ds(pl.multiple_of(side * half, half), half), :]
    product = jnp.dot(grad, factor, preferred_element_type=jnp.float32)
    grad_float = grad.astype(jnp.float32)
    return product, jnp.sum(grad_float * grad_float, keepdims=True)


def own_product_kernel(core_ref, own_ref, right_ref, product_ref, squares_ref):
    product, squares = half_product(core_ref, own_ref, right_ref, False)
    product_ref[...] = product
    squares_ref[...] = jnp.broadcast_to(squares, squares_ref.shape)


def own_product(core, own, right_root):
    return pl.pallas_call(
        own_product_kernel,
        out_shape=(
            jax.ShapeDtypeStruct(right_root.shape, jnp.float32),
            jax.ShapeDtypeStruct((1, LANES), jnp.float32),
        ),
        in_specs=[SMEM, VMEM, VMEM],
        out_specs=(VMEM, VMEM),
        compiler_params=pltpu.CompilerParams(vmem_limit_bytes=32 * 2**20),
        name="own_product",
    )(core.reshape(1), own, right_root)


def precondition_kernel(
    core_ref, product_ref, squares_ref, other_ref, left_ref, right_ref, out_ref
):
    size = left_ref.shape[-1]
    half = other_ref.shape[-1]
    area = float(size * size)
    product, squares = half_product(core_ref, other_ref, right_ref, True)
    right_prod = (product_ref[...] + product).astype(jnp.bfloat16)
    grad_squares = squares_ref[:, :1] + squares
    precond = jnp.dot(left_ref[...], right_prod, preferred_element_type=jnp.float32)
    precond_squares = jnp.sum(precond * precond, keepdims=True)
    scale = jnp.sqrt(grad_squares / area) / jnp.sqrt(precond_squares / area + 1e-06)
    grafted = (precond[:, :half] * scale).astype(out_ref.dtype)
    out_ref[...] = grafted.reshape(out_ref.shape)


def precondition(core, product, squares, other, left_root, right_root):
    return pl.pallas_call(
        precondition_kernel,
        out_shape=jax.ShapeDtypeStruct(other.shape, other.dtype),
        in_specs=[SMEM, VMEM, VMEM, VMEM, VMEM, VMEM],
        out_specs=VMEM,
        compiler_params=pltpu.CompilerParams(vmem_limit_bytes=32 * 2**20),
        name="precondition",
    )(core.reshape(1), product, squares, other, left_root, right_root)


def split_columns_kernel(owner_ref, rows_ref, out_ref):
    replicas, groups, rows, lanes = out_ref.shape
    width = rows_ref.shape[-1] // replicas
    per = lanes // width
    lane = lax.broadcasted_iota(jnp.int32, (rows, lanes), 1) // width
    for g in range(groups):
        blocks = [rows_ref[owner_ref[g * per + i]].astype(jnp.float32) for i in range(per)]
        for t in range(replicas // per):
            tiles = [block[:, t * lanes : (t + 1) * lanes] for block in blocks]
            for k in range(per):
                mixed = tiles[k]
                for i in range(per):
                    if i != k:
                        moved = pltpu.roll(tiles[i], ((i - k) % per) * width, 1)
                        mixed = jnp.where(lane == i, moved, mixed)
                out_ref[t * per + k, g] = mixed.astype(out_ref.dtype)


def split_columns(owner, rows, replicas):
    count = owner.shape[0]
    width = rows.shape[-1] // replicas
    per = LANES // width
    shape = (replicas, count // per, rows.shape[1], LANES)
    return pl.pallas_call(
        split_columns_kernel,
        out_shape=jax.ShapeDtypeStruct(shape, rows.dtype),
        in_specs=[SMEM, VMEM],
        out_specs=VMEM,
        compiler_params=pltpu.CompilerParams(vmem_limit_bytes=32 * 2**20),
        name="split_columns",
    )(owner, rows)


def update_kernel(place_ref, momentum_ref, pieces_ref, out_ref):
    replicas, groups, rows, lanes = pieces_ref.shape
    width, count = momentum_ref.shape[1:]
    per = lanes // width
    depth = replicas * groups * rows
    flipped = pieces_ref[...].astype(jnp.float32).reshape(depth, lanes).T.astype(jnp.bfloat16)
    place = place_ref[...]
    group = place // per
    turn = place % per
    source = lax.broadcasted_iota(jnp.int32, (depth, count), 0) - group * rows
    for row in range(rows):
        pick = (source == row).astype(jnp.bfloat16)
        spread = jnp.dot(flipped, pick, preferred_element_type=jnp.float32)
        value = jnp.zeros((width, count), jnp.float32)
        for i in range(per):
            value = jnp.where(turn == i, spread[i * width : (i + 1) * width], value)
        out_ref[row] = 0.9 * momentum_ref[row] + 0.1 * value


def update(place, momentum, pieces):
    flipped = pl.pallas_call(
        update_kernel,
        out_shape=jax.ShapeDtypeStruct(
            (momentum.shape[1], momentum.shape[2], momentum.shape[0]), momentum.dtype
        ),
        in_specs=[VMEM, VMEM, VMEM],
        out_specs=VMEM,
        compiler_params=pltpu.CompilerParams(vmem_limit_bytes=32 * 2**20),
        name="update",
    )(place.reshape(1, -1), jnp.transpose(momentum, (1, 2, 0)), pieces)
    return jnp.transpose(flipped, (2, 0, 1))


def neighbour(place):
    x, core = place // 2, place % 2
    step = 1 if (x + core) % 2 == 0 else -1
    return (x + step) % 8 * 2 + core


def on_device(partial_grads, block_owner, block_slot, left_roots, right_roots, momentum):
    along_x = ("xh", "xl")
    rep = along_x + ("core",)
    fsdp = ("y", "z")
    owner_count = lax.axis_size(fsdp)
    planes = lax.axis_size(along_x)
    pairs = lax.axis_size("xh")
    cores = lax.axis_size("core")
    most = left_roots.shape[0]
    blocks, rows, width = partial_grads.shape[1:]
    each = blocks // planes
    half = width // cores
    core = lax.axis_index("core")
    plane = lax.axis_index(along_x).astype(jnp.uint32)
    parity = lax.axis_index("xl").astype(jnp.uint32)
    me = lax.axis_index(fsdp)

    swap = [(i, 1 - i) for i in range(cores)]
    grads = pltpu.with_memory_space_constraint(partial_grads[0], pltpu.HBM)
    away = column_half(1 - core, grads)
    other = lax.ppermute(away, "core", swap)
    core_later, away = lax.optimization_barrier((core, away))
    own = column_half(core_later, grads)

    entry = block_owner * most + block_slot
    rank = jnp.sum((entry[None, :] < entry[:, None]).astype(jnp.uint32), axis=1)
    block_plane = rank % planes
    turn = rank // planes
    spot = ((block_plane + parity) % 2 * pairs + block_plane // 2) * each + turn
    order = lax.iota(jnp.uint32, blocks)
    block_at = jnp.sum(jnp.where(spot[None, :] == order[:, None], order[None, :], 0), axis=1)
    keep, away = pair_sum(block_at.astype(jnp.int32), own, other)

    away, rank = lax.optimization_barrier((away, rank))
    met = lax.ppermute(away, rep, [(i, neighbour(i)) for i in range(planes * cores)])
    place = (rank % planes * each + rank // planes).astype(jnp.int32)
    turns = lax.broadcasted_iota(jnp.uint32, (each, blocks), 0)
    turn_is = rank[None] == turns * planes + plane
    my_owner = jnp.sum(jnp.where(turn_is, block_owner[None], 0), axis=1)
    mine = (rank % planes == plane) & (block_owner == me)
    my_slot = jnp.sum(jnp.where(mine, block_slot, 0))
    left_root, right_root = fetch_roots(my_slot, core, left_roots, right_roots, half // planes)
    met, left_root, right_root, my_owner, place = lax.optimization_barrier(
        (met, left_root, right_root, my_owner, place)
    )

    parts = lax.all_to_all(
        (keep + met).reshape(pairs, each, rows, half), "xh", split_axis=0, concat_axis=0, tiled=True
    )
    to_owner = sum_to_owner(my_owner, parts, owner_count)
    grad_half = lax.all_to_all(to_owner, fsdp, split_axis=0, concat_axis=0, tiled=True)
    other_half = lax.ppermute(grad_half, "core", swap)
    product, squares = own_product(core, grad_half, right_root)
    grafted = precondition(core, product, squares, other_half, left_root, right_root)
    back = lax.all_to_all(grafted, fsdp, split_axis=0, concat_axis=0, tiled=True)
    pieces = split_columns(my_owner, back, planes)
    pieces = lax.all_to_all(pieces, along_x, split_axis=0, concat_axis=0, tiled=True)
    return update(place, momentum, pieces)


def solution(mesh):
    devices = mesh.devices.reshape(4, 2, 2, 8, 8)
    split = Mesh(devices, ("xh", "xl", "core", "y", "z"))
    rep, fsdp = ("xh", "xl", "core"), ("y", "z")
    in_specs = (
        P(rep, None, fsdp, None),
        P(),
        P(),
        P(fsdp, None, None),
        P(fsdp, None, None),
        P(None, fsdp, rep),
    )
    out_specs = P(None, fsdp, rep)
    return jax.shard_map(
        on_device, mesh=split, in_specs=in_specs, out_specs=out_specs, check_vma=False
    )
```

```python
import functools

import jax
import jax.numpy as jnp
from jax import lax
from jax.experimental import pallas as pl
from jax.experimental.pallas import tpu as pltpu
from jax.sharding import Mesh, PartitionSpec as P

LANES = 128
COPIES = 4
VMEM = pl.BlockSpec(memory_space=pltpu.VMEM)
SMEM = pl.BlockSpec(memory_space=pltpu.SMEM)


def column_half_kernel(side_ref, grads_ref, half_ref, sems):
    width = half_ref.shape[2]
    parts = sems.shape[0]
    count = half_ref.shape[0] // parts
    columns = pl.ds(pl.multiple_of(side_ref[0] * width, width), width)
    copies = [
        pltpu.make_async_copy(
            grads_ref.at[pl.ds(i * count, count), :, columns],
            half_ref.at[pl.ds(i * count, count)],
            sems.at[i],
        )
        for i in range(parts)
    ]
    for copy in copies:
        copy.start()
    for copy in copies:
        copy.wait()


def column_half(side, grads):
    blocks, rows, width = grads.shape
    return pl.pallas_call(
        column_half_kernel,
        out_shape=jax.ShapeDtypeStruct((blocks, rows, width // 2), grads.dtype),
        in_specs=[SMEM, pl.BlockSpec(memory_space=pltpu.HBM)],
        out_specs=VMEM,
        scratch_shapes=[pltpu.SemaphoreType.DMA((COPIES,))],
        compiler_params=pltpu.CompilerParams(vmem_limit_bytes=32 * 2**20),
        name="column_half",
    )(side.reshape(1), grads)


def pair_sum_kernel(first, block_ref, own_ref, other_ref, out_ref):
    for p in range(out_ref.shape[0]):
        b = block_ref[first + p]
        out_ref[p] = own_ref[b] + other_ref[b]


def pair_sum(block_at, own, other, first, count):
    return pl.pallas_call(
        functools.partial(pair_sum_kernel, first),
        out_shape=jax.ShapeDtypeStruct((count,) + own.shape[1:], own.dtype),
        in_specs=[SMEM, VMEM, VMEM],
        out_specs=VMEM,
        compiler_params=pltpu.CompilerParams(vmem_limit_bytes=32 * 2**20),
        name="pair_sum",
    )(block_at, own, other)


def sum_to_owner_kernel(owner_ref, parts_ref, out_ref):
    out_ref[...] = jnp.zeros_like(out_ref)
    for j in range(parts_ref.shape[1]):
        total = parts_ref[0, j].astype(jnp.float32)
        for i in range(1, parts_ref.shape[0]):
            total = total + parts_ref[i, j].astype(jnp.float32)
        out_ref[owner_ref[j]] = total.astype(out_ref.dtype)


def sum_to_owner(owner, parts, owner_count):
    return pl.pallas_call(
        sum_to_owner_kernel,
        out_shape=jax.ShapeDtypeStruct((owner_count,) + parts.shape[2:], parts.dtype),
        in_specs=[SMEM, VMEM],
        out_specs=VMEM,
        compiler_params=pltpu.CompilerParams(vmem_limit_bytes=32 * 2**20),
        name="sum_to_owner",
    )(owner, parts)


def fetch_roots_kernel(
    slot_ref, core_ref, left_table, right_table, left_ref, right_ref, raw_ref, sems, *, slice_cols
):
    slot = slot_ref[0]
    left_copy = pltpu.make_async_copy(left_table.at[slot], left_ref, sems.at[0])
    right_copy = pltpu.make_async_copy(right_table.at[slot], raw_ref, sems.at[1])
    right_copy.start()
    left_copy.start()
    size = raw_ref.shape[0]
    half = size // 2
    column = lax.broadcasted_iota(jnp.int32, (size, size), 1)
    inner = column % half
    side = jnp.where(column < half, core_ref[0], 1 - core_ref[0])
    source = inner // slice_cols * (2 * slice_cols) + side * slice_cols + inner % slice_cols
    pick = (lax.broadcasted_iota(jnp.int32, (size, size), 0) == source).astype(jnp.bfloat16)
    right_copy.wait()
    ordered = jnp.dot(raw_ref[...], pick, preferred_element_type=jnp.float32)
    right_ref[...] = ordered.astype(right_ref.dtype)
    left_copy.wait()


def fetch_roots(slot, core, left_roots, right_roots, slice_cols):
    root = jax.ShapeDtypeStruct(left_roots.shape[1:], left_roots.dtype)
    hbm = pl.BlockSpec(memory_space=pltpu.HBM)
    return pl.pallas_call(
        functools.partial(fetch_roots_kernel, slice_cols=slice_cols),
        out_shape=(root, root),
        in_specs=[SMEM, SMEM, hbm, hbm],
        out_specs=(VMEM, VMEM),
        scratch_shapes=[
            pltpu.VMEM(root.shape, root.dtype),
            pltpu.SemaphoreType.DMA((2,)),
        ],
        compiler_params=pltpu.CompilerParams(vmem_limit_bytes=32 * 2**20),
        name="fetch_roots",
    )(
        slot.reshape(1),
        core.reshape(1),
        pltpu.with_memory_space_constraint(left_roots, pltpu.HBM),
        pltpu.with_memory_space_constraint(right_roots, pltpu.HBM),
    )


def half_product(core_ref, grad_ref, right_ref, opposite):
    size, half = right_ref.shape[0], grad_ref.shape[-1]
    side = 1 - core_ref[0] if opposite else core_ref[0]
    grad = grad_ref[...].reshape(size, half)
    factor = right_ref[pl.ds(pl.multiple_of(side * half, half), half), :]
    product = jnp.dot(grad, factor, preferred_element_type=jnp.float32)
    grad_float = grad.astype(jnp.float32)
    return product, jnp.sum(grad_float * grad_float, keepdims=True)


def own_product_kernel(core_ref, own_ref, right_ref, product_ref, squares_ref):
    product, squares = half_product(core_ref, own_ref, right_ref, False)
    product_ref[...] = product
    squares_ref[...] = jnp.broadcast_to(squares, squares_ref.shape)


def own_product(core, own, right_root):
    return pl.pallas_call(
        own_product_kernel,
        out_shape=(
            jax.ShapeDtypeStruct(right_root.shape, jnp.float32),
            jax.ShapeDtypeStruct((1, LANES), jnp.float32),
        ),
        in_specs=[SMEM, VMEM, VMEM],
        out_specs=(VMEM, VMEM),
        compiler_params=pltpu.CompilerParams(vmem_limit_bytes=32 * 2**20),
        name="own_product",
    )(core.reshape(1), own, right_root)


def precondition_kernel(
    core_ref, product_ref, squares_ref, other_ref, left_ref, right_ref, out_ref
):
    size = left_ref.shape[-1]
    half = other_ref.shape[-1]
    area = float(size * size)
    product, squares = half_product(core_ref, other_ref, right_ref, True)
    right_prod = (product_ref[...] + product).astype(jnp.bfloat16)
    grad_squares = squares_ref[:, :1] + squares
    precond = jnp.dot(left_ref[...], right_prod, preferred_element_type=jnp.float32)
    precond_squares = jnp.sum(precond * precond, keepdims=True)
    scale = jnp.sqrt(grad_squares / area) / jnp.sqrt(precond_squares / area + 1e-06)
    grafted = (precond[:, :half] * scale).astype(out_ref.dtype)
    out_ref[...] = grafted.reshape(out_ref.shape)


def precondition(core, product, squares, other, left_root, right_root):
    return pl.pallas_call(
        precondition_kernel,
        out_shape=jax.ShapeDtypeStruct(other.shape, other.dtype),
        in_specs=[SMEM, VMEM, VMEM, VMEM, VMEM, VMEM],
        out_specs=VMEM,
        compiler_params=pltpu.CompilerParams(vmem_limit_bytes=32 * 2**20),
        name="precondition",
    )(core.reshape(1), product, squares, other, left_root, right_root)


def split_columns_kernel(owner_ref, rows_ref, out_ref):
    replicas, groups, rows, lanes = out_ref.shape
    width = rows_ref.shape[-1] // replicas
    per = lanes // width
    lane = lax.broadcasted_iota(jnp.int32, (rows, lanes), 1) // width
    for g in range(groups):
        blocks = [rows_ref[owner_ref[g * per + i]].astype(jnp.float32) for i in range(per)]
        for t in range(replicas // per):
            tiles = [block[:, t * lanes : (t + 1) * lanes] for block in blocks]
            for k in range(per):
                mixed = tiles[k]
                for i in range(per):
                    if i != k:
                        moved = pltpu.roll(tiles[i], ((i - k) % per) * width, 1)
                        mixed = jnp.where(lane == i, moved, mixed)
                out_ref[t * per + k, g] = mixed.astype(out_ref.dtype)


def split_columns(owner, rows, replicas):
    count = owner.shape[0]
    width = rows.shape[-1] // replicas
    per = LANES // width
    shape = (replicas, count // per, rows.shape[1], LANES)
    return pl.pallas_call(
        split_columns_kernel,
        out_shape=jax.ShapeDtypeStruct(shape, rows.dtype),
        in_specs=[SMEM, VMEM],
        out_specs=VMEM,
        compiler_params=pltpu.CompilerParams(vmem_limit_bytes=32 * 2**20),
        name="split_columns",
    )(owner, rows)


def update_kernel(place_ref, momentum_ref, pieces_ref, out_ref):
    replicas, groups, rows, lanes = pieces_ref.shape
    width, count = momentum_ref.shape[1:]
    per = lanes // width
    depth = replicas * groups * rows
    flipped = pieces_ref[...].astype(jnp.float32).reshape(depth, lanes).T.astype(jnp.bfloat16)
    place = place_ref[...]
    group = place // per
    turn = place % per
    source = lax.broadcasted_iota(jnp.int32, (depth, count), 0) - group * rows
    for row in range(rows):
        pick = (source == row).astype(jnp.bfloat16)
        spread = jnp.dot(flipped, pick, preferred_element_type=jnp.float32)
        value = jnp.zeros((width, count), jnp.float32)
        for i in range(per):
            value = jnp.where(turn == i, spread[i * width : (i + 1) * width], value)
        out_ref[row] = 0.9 * momentum_ref[row] + 0.1 * value


def update(place, momentum, pieces):
    flipped = pl.pallas_call(
        update_kernel,
        out_shape=jax.ShapeDtypeStruct(
            (momentum.shape[1], momentum.shape[2], momentum.shape[0]), momentum.dtype
        ),
        in_specs=[VMEM, VMEM, VMEM],
        out_specs=VMEM,
        compiler_params=pltpu.CompilerParams(vmem_limit_bytes=32 * 2**20),
        name="update",
    )(place.reshape(1, -1), jnp.transpose(momentum, (1, 2, 0)), pieces)
    return jnp.transpose(flipped, (2, 0, 1))


def neighbour(place):
    x, core = place // 2, place % 2
    step = 1 if (x + core) % 2 == 0 else -1
    return (x + step) % 8 * 2 + core


def on_device(partial_grads, block_owner, block_slot, left_roots, right_roots, momentum):
    along_x = ("xh", "xl")
    rep = along_x + ("core",)
    fsdp = ("y", "z")
    owner_count = lax.axis_size(fsdp)
    planes = lax.axis_size(along_x)
    pairs = lax.axis_size("xh")
    cores = lax.axis_size("core")
    most = left_roots.shape[0]
    blocks, rows, width = partial_grads.shape[1:]
    each = blocks // planes
    half = width // cores
    core = lax.axis_index("core")
    plane = lax.axis_index(along_x).astype(jnp.uint32)
    parity = lax.axis_index("xl").astype(jnp.uint32)
    me = lax.axis_index(fsdp)

    swap = [(i, 1 - i) for i in range(cores)]
    grads = pltpu.with_memory_space_constraint(partial_grads[0], pltpu.HBM)
    away = column_half(1 - core, grads)
    other = lax.ppermute(away, "core", swap)
    core_later, away = lax.optimization_barrier((core, away))
    own = column_half(core_later, grads)
    own, owner_later, slot_later = lax.optimization_barrier((own, block_owner, block_slot))

    entry = owner_later * most + slot_later
    rank = jnp.sum((entry[None, :] < entry[:, None]).astype(jnp.uint32), axis=1)
    block_plane = rank % planes
    turn = rank // planes
    spot = ((block_plane + parity) % 2 * pairs + block_plane // 2) * each + turn
    order = lax.iota(jnp.uint32, blocks)
    block_at = jnp.sum(jnp.where(spot[None, :] == order[:, None], order[None, :], 0), axis=1)
    block_at = block_at.astype(jnp.int32)
    away = pair_sum(block_at, own, other, blocks // 2, blocks // 2)

    away, rank, block_at = lax.optimization_barrier((away, rank, block_at))
    keep = pair_sum(block_at, own, other, 0, blocks // 2)
    met = lax.ppermute(away, rep, [(i, neighbour(i)) for i in range(planes * cores)])
    place = (rank % planes * each + rank // planes).astype(jnp.int32)
    turns = lax.broadcasted_iota(jnp.uint32, (each, blocks), 0)
    turn_is = rank[None] == turns * planes + plane
    my_owner = jnp.sum(jnp.where(turn_is, block_owner[None], 0), axis=1)
    mine = (rank % planes == plane) & (block_owner == me)
    my_slot = jnp.sum(jnp.where(mine, block_slot, 0))
    left_root, right_root = fetch_roots(my_slot, core, left_roots, right_roots, half // planes)
    met, keep, left_root, right_root, my_owner, place = lax.optimization_barrier(
        (met, keep, left_root, right_root, my_owner, place)
    )

    parts = lax.all_to_all(
        (keep + met).reshape(pairs, each, rows, half), "xh", split_axis=0, concat_axis=0, tiled=True
    )
    to_owner = sum_to_owner(my_owner, parts, owner_count)
    grad_half = lax.all_to_all(to_owner, fsdp, split_axis=0, concat_axis=0, tiled=True)
    other_half = lax.ppermute(grad_half, "core", swap)
    product, squares = own_product(core, grad_half, right_root)
    grafted = precondition(core, product, squares, other_half, left_root, right_root)
    back = lax.all_to_all(grafted, fsdp, split_axis=0, concat_axis=0, tiled=True)
    pieces = split_columns(my_owner, back, planes)
    pieces = lax.all_to_all(pieces, along_x, split_axis=0, concat_axis=0, tiled=True)
    return update(place, momentum, pieces)


def solution(mesh):
    devices = mesh.devices.reshape(4, 2, 2, 8, 8)
    split = Mesh(devices, ("xh", "xl", "core", "y", "z"))
    rep, fsdp = ("xh", "xl", "core"), ("y", "z")
    in_specs = (
        P(rep, None, fsdp, None),
        P(),
        P(),
        P(fsdp, None, None),
        P(fsdp, None, None),
        P(None, fsdp, rep),
    )
    out_specs = P(None, fsdp, rep)
    return jax.shard_map(
        on_device, mesh=split, in_specs=in_specs, out_specs=out_specs, check_vma=False
    )
```

```python
import functools

import jax
import jax.numpy as jnp
from jax import lax
from jax.experimental import pallas as pl
from jax.experimental.pallas import tpu as pltpu
from jax.sharding import Mesh, PartitionSpec as P

LANES = 128
COPIES = 4
VMEM = pl.BlockSpec(memory_space=pltpu.VMEM)
SMEM = pl.BlockSpec(memory_space=pltpu.SMEM)


def column_half_kernel(side_ref, grads_ref, half_ref, sems):
    width = half_ref.shape[2]
    parts = sems.shape[0]
    count = half_ref.shape[0] // parts
    columns = pl.ds(pl.multiple_of(side_ref[0] * width, width), width)
    copies = [
        pltpu.make_async_copy(
            grads_ref.at[pl.ds(i * count, count), :, columns],
            half_ref.at[pl.ds(i * count, count)],
            sems.at[i],
        )
        for i in range(parts)
    ]
    for copy in copies:
        copy.start()
    for copy in copies:
        copy.wait()


def column_half(side, grads):
    blocks, rows, width = grads.shape
    return pl.pallas_call(
        column_half_kernel,
        out_shape=jax.ShapeDtypeStruct((blocks, rows, width // 2), grads.dtype),
        in_specs=[SMEM, pl.BlockSpec(memory_space=pltpu.HBM)],
        out_specs=VMEM,
        scratch_shapes=[pltpu.SemaphoreType.DMA((COPIES,))],
        compiler_params=pltpu.CompilerParams(vmem_limit_bytes=32 * 2**20),
        name="column_half",
    )(side.reshape(1), grads)


def pair_sum_kernel(first, core_ref, block_ref, own_ref, other_ref, out_ref):
    width = own_ref.shape[2]
    columns = pl.ds(pl.multiple_of(core_ref[0] * width, width), width)
    for p in range(out_ref.shape[0]):
        b = block_ref[first + p]
        out_ref[p] = own_ref[b] + other_ref[b, :, columns]


def pair_sum(core, block_at, own, other, first, count):
    return pl.pallas_call(
        functools.partial(pair_sum_kernel, first),
        out_shape=jax.ShapeDtypeStruct((count,) + own.shape[1:], own.dtype),
        in_specs=[SMEM, SMEM, VMEM, VMEM],
        out_specs=VMEM,
        compiler_params=pltpu.CompilerParams(vmem_limit_bytes=32 * 2**20),
        name="pair_sum",
    )(core.reshape(1), block_at, own, other)


def sum_to_owner_kernel(owner_ref, parts_ref, out_ref):
    out_ref[...] = jnp.zeros_like(out_ref)
    for j in range(parts_ref.shape[1]):
        total = parts_ref[0, j].astype(jnp.float32)
        for i in range(1, parts_ref.shape[0]):
            total = total + parts_ref[i, j].astype(jnp.float32)
        out_ref[owner_ref[j]] = total.astype(out_ref.dtype)


def sum_to_owner(owner, parts, owner_count):
    return pl.pallas_call(
        sum_to_owner_kernel,
        out_shape=jax.ShapeDtypeStruct((owner_count,) + parts.shape[2:], parts.dtype),
        in_specs=[SMEM, VMEM],
        out_specs=VMEM,
        compiler_params=pltpu.CompilerParams(vmem_limit_bytes=32 * 2**20),
        name="sum_to_owner",
    )(owner, parts)


def fetch_roots_kernel(
    slot_ref, core_ref, left_table, right_table, left_ref, right_ref, raw_ref, sems, *, slice_cols
):
    slot = slot_ref[0]
    left_copy = pltpu.make_async_copy(left_table.at[slot], left_ref, sems.at[0])
    right_copy = pltpu.make_async_copy(right_table.at[slot], raw_ref, sems.at[1])
    right_copy.start()
    left_copy.start()
    size = raw_ref.shape[0]
    half = size // 2
    column = lax.broadcasted_iota(jnp.int32, (size, size), 1)
    inner = column % half
    side = jnp.where(column < half, core_ref[0], 1 - core_ref[0])
    source = inner // slice_cols * (2 * slice_cols) + side * slice_cols + inner % slice_cols
    pick = (lax.broadcasted_iota(jnp.int32, (size, size), 0) == source).astype(jnp.bfloat16)
    right_copy.wait()
    ordered = jnp.dot(raw_ref[...], pick, preferred_element_type=jnp.float32)
    right_ref[...] = ordered.astype(right_ref.dtype)
    left_copy.wait()


def fetch_roots(slot, core, left_roots, right_roots, slice_cols):
    root = jax.ShapeDtypeStruct(left_roots.shape[1:], left_roots.dtype)
    hbm = pl.BlockSpec(memory_space=pltpu.HBM)
    return pl.pallas_call(
        functools.partial(fetch_roots_kernel, slice_cols=slice_cols),
        out_shape=(root, root),
        in_specs=[SMEM, SMEM, hbm, hbm],
        out_specs=(VMEM, VMEM),
        scratch_shapes=[
            pltpu.VMEM(root.shape, root.dtype),
            pltpu.SemaphoreType.DMA((2,)),
        ],
        compiler_params=pltpu.CompilerParams(vmem_limit_bytes=32 * 2**20),
        name="fetch_roots",
    )(
        slot.reshape(1),
        core.reshape(1),
        pltpu.with_memory_space_constraint(left_roots, pltpu.HBM),
        pltpu.with_memory_space_constraint(right_roots, pltpu.HBM),
    )


def half_product(core_ref, grad_ref, right_ref, opposite):
    size, half = right_ref.shape[0], grad_ref.shape[-1]
    side = 1 - core_ref[0] if opposite else core_ref[0]
    grad = grad_ref[...].reshape(size, half)
    factor = right_ref[pl.ds(pl.multiple_of(side * half, half), half), :]
    product = jnp.dot(grad, factor, preferred_element_type=jnp.float32)
    grad_float = grad.astype(jnp.float32)
    return product, jnp.sum(grad_float * grad_float, keepdims=True)


def own_product_kernel(core_ref, own_ref, right_ref, product_ref, squares_ref):
    product, squares = half_product(core_ref, own_ref, right_ref, False)
    product_ref[...] = product
    squares_ref[...] = jnp.broadcast_to(squares, squares_ref.shape)


def own_product(core, own, right_root):
    return pl.pallas_call(
        own_product_kernel,
        out_shape=(
            jax.ShapeDtypeStruct(right_root.shape, jnp.float32),
            jax.ShapeDtypeStruct((1, LANES), jnp.float32),
        ),
        in_specs=[SMEM, VMEM, VMEM],
        out_specs=(VMEM, VMEM),
        compiler_params=pltpu.CompilerParams(vmem_limit_bytes=32 * 2**20),
        name="own_product",
    )(core.reshape(1), own, right_root)


def precondition_kernel(
    core_ref, product_ref, squares_ref, other_ref, left_ref, right_ref, out_ref
):
    size = left_ref.shape[-1]
    half = other_ref.shape[-1]
    area = float(size * size)
    product, squares = half_product(core_ref, other_ref, right_ref, True)
    right_prod = (product_ref[...] + product).astype(jnp.bfloat16)
    grad_squares = squares_ref[:, :1] + squares
    precond = jnp.dot(left_ref[...], right_prod, preferred_element_type=jnp.float32)
    precond_squares = jnp.sum(precond * precond, keepdims=True)
    scale = jnp.sqrt(grad_squares / area) / jnp.sqrt(precond_squares / area + 1e-06)
    grafted = (precond[:, :half] * scale).astype(out_ref.dtype)
    out_ref[...] = grafted.reshape(out_ref.shape)


def precondition(core, product, squares, other, left_root, right_root):
    return pl.pallas_call(
        precondition_kernel,
        out_shape=jax.ShapeDtypeStruct(other.shape, other.dtype),
        in_specs=[SMEM, VMEM, VMEM, VMEM, VMEM, VMEM],
        out_specs=VMEM,
        compiler_params=pltpu.CompilerParams(vmem_limit_bytes=32 * 2**20),
        name="precondition",
    )(core.reshape(1), product, squares, other, left_root, right_root)


def split_columns_kernel(owner_ref, rows_ref, out_ref):
    replicas, groups, rows, lanes = out_ref.shape
    width = rows_ref.shape[-1] // replicas
    per = lanes // width
    lane = lax.broadcasted_iota(jnp.int32, (rows, lanes), 1) // width
    for g in range(groups):
        blocks = [rows_ref[owner_ref[g * per + i]].astype(jnp.float32) for i in range(per)]
        for t in range(replicas // per):
            tiles = [block[:, t * lanes : (t + 1) * lanes] for block in blocks]
            for k in range(per):
                mixed = tiles[k]
                for i in range(per):
                    if i != k:
                        moved = pltpu.roll(tiles[i], ((i - k) % per) * width, 1)
                        mixed = jnp.where(lane == i, moved, mixed)
                out_ref[t * per + k, g] = mixed.astype(out_ref.dtype)


def split_columns(owner, rows, replicas):
    count = owner.shape[0]
    width = rows.shape[-1] // replicas
    per = LANES // width
    shape = (replicas, count // per, rows.shape[1], LANES)
    return pl.pallas_call(
        split_columns_kernel,
        out_shape=jax.ShapeDtypeStruct(shape, rows.dtype),
        in_specs=[SMEM, VMEM],
        out_specs=VMEM,
        compiler_params=pltpu.CompilerParams(vmem_limit_bytes=32 * 2**20),
        name="split_columns",
    )(owner, rows)


def update_kernel(place_ref, momentum_ref, pieces_ref, out_ref, rows_ref):
    replicas, groups, rows, lanes = pieces_ref.shape
    width, count = momentum_ref.shape[1:]
    per = lanes // width
    depth = replicas * groups
    rows_ref[...] = pieces_ref[...].astype(jnp.float32).reshape(depth * rows, lanes)
    place = place_ref[...]
    turn = place % per
    group = lax.broadcasted_iota(jnp.int32, (depth, count), 0)
    pick = (group == place // per).astype(jnp.bfloat16)
    for row in range(rows):
        flipped = rows_ref[pl.ds(row, depth, stride=rows), :].T.astype(jnp.bfloat16)
        spread = jnp.dot(flipped, pick, preferred_element_type=jnp.float32)
        value = jnp.zeros((width, count), jnp.float32)
        for i in range(per):
            value = jnp.where(turn == i, spread[i * width : (i + 1) * width], value)
        out_ref[row] = 0.9 * momentum_ref[row] + 0.1 * value


def update(place, momentum, pieces):
    replicas, groups, rows, lanes = pieces.shape
    flipped = pl.pallas_call(
        update_kernel,
        out_shape=jax.ShapeDtypeStruct(
            (momentum.shape[1], momentum.shape[2], momentum.shape[0]), momentum.dtype
        ),
        in_specs=[VMEM, VMEM, VMEM],
        out_specs=VMEM,
        scratch_shapes=[pltpu.VMEM((replicas * groups * rows, lanes), jnp.float32)],
        compiler_params=pltpu.CompilerParams(vmem_limit_bytes=32 * 2**20),
        name="update",
    )(place.reshape(1, -1), jnp.transpose(momentum, (1, 2, 0)), pieces)
    return jnp.transpose(flipped, (2, 0, 1))


def neighbour(place):
    x, core = place // 2, place % 2
    step = 1 if (x + core) % 2 == 0 else -1
    return (x + step) % 8 * 2 + core


def on_device(partial_grads, block_owner, block_slot, left_roots, right_roots, momentum):
    along_x = ("xh", "xl")
    rep = along_x + ("core",)
    fsdp = ("y", "z")
    owner_count = lax.axis_size(fsdp)
    planes = lax.axis_size(along_x)
    pairs = lax.axis_size("xh")
    cores = lax.axis_size("core")
    most = left_roots.shape[0]
    blocks, rows, width = partial_grads.shape[1:]
    each = blocks // planes
    half = width // cores
    core = lax.axis_index("core")
    plane = lax.axis_index(along_x).astype(jnp.uint32)
    parity = lax.axis_index("xl").astype(jnp.uint32)
    me = lax.axis_index(fsdp)

    swap = [(i, 1 - i) for i in range(cores)]
    other = lax.ppermute(partial_grads[0], "core", swap)
    own = column_half(core, pltpu.with_memory_space_constraint(partial_grads[0], pltpu.HBM))
    own, owner_later, slot_later = lax.optimization_barrier((own, block_owner, block_slot))

    entry = owner_later * most + slot_later
    rank = jnp.sum((entry[None, :] < entry[:, None]).astype(jnp.uint32), axis=1)
    block_plane = rank % planes
    turn = rank // planes
    spot = ((block_plane + parity) % 2 * pairs + block_plane // 2) * each + turn
    order = lax.iota(jnp.uint32, blocks)
    block_at = jnp.sum(jnp.where(spot[None, :] == order[:, None], order[None, :], 0), axis=1)
    block_at = block_at.astype(jnp.int32)
    away = pair_sum(core, block_at, own, other, blocks // 2, blocks // 2)

    away, rank, block_at = lax.optimization_barrier((away, rank, block_at))
    keep = pair_sum(core, block_at, own, other, 0, blocks // 2)
    met = lax.ppermute(away, rep, [(i, neighbour(i)) for i in range(planes * cores)])
    place = (rank % planes * each + rank // planes).astype(jnp.int32)
    turns = lax.broadcasted_iota(jnp.uint32, (each, blocks), 0)
    turn_is = rank[None] == turns * planes + plane
    my_owner = jnp.sum(jnp.where(turn_is, block_owner[None], 0), axis=1)
    mine = (rank % planes == plane) & (block_owner == me)
    my_slot = jnp.sum(jnp.where(mine, block_slot, 0))
    left_root, right_root = fetch_roots(my_slot, core, left_roots, right_roots, half // planes)
    met, keep, left_root, right_root, my_owner, place = lax.optimization_barrier(
        (met, keep, left_root, right_root, my_owner, place)
    )

    parts = lax.all_to_all(
        (keep + met).reshape(pairs, each, rows, half), "xh", split_axis=0, concat_axis=0, tiled=True
    )
    to_owner = sum_to_owner(my_owner, parts, owner_count)
    grad_half = lax.all_to_all(to_owner, fsdp, split_axis=0, concat_axis=0, tiled=True)
    other_half = lax.ppermute(grad_half, "core", swap)
    product, squares = own_product(core, grad_half, right_root)
    grafted = precondition(core, product, squares, other_half, left_root, right_root)
    back = lax.all_to_all(grafted, fsdp, split_axis=0, concat_axis=0, tiled=True)
    pieces = split_columns(my_owner, back, planes)
    pieces = lax.all_to_all(pieces, along_x, split_axis=0, concat_axis=0, tiled=True)
    return update(place, momentum, pieces)


def solution(mesh):
    devices = mesh.devices.reshape(4, 2, 2, 8, 8)
    split = Mesh(devices, ("xh", "xl", "core", "y", "z"))
    rep, fsdp = ("xh", "xl", "core"), ("y", "z")
    in_specs = (
        P(rep, None, fsdp, None),
        P(),
        P(),
        P(fsdp, None, None),
        P(fsdp, None, None),
        P(None, fsdp, rep),
    )
    out_specs = P(None, fsdp, rep)
    return jax.shard_map(
        on_device, mesh=split, in_specs=in_specs, out_specs=out_specs, check_vma=False
    )
```

```python
import functools

import jax
import jax.numpy as jnp
from jax import lax
from jax.experimental import pallas as pl
from jax.experimental.pallas import tpu as pltpu
from jax.sharding import Mesh, PartitionSpec as P

LANES = 128
COPIES = 4
VMEM = pl.BlockSpec(memory_space=pltpu.VMEM)
SMEM = pl.BlockSpec(memory_space=pltpu.SMEM)


def column_half_kernel(side_ref, grads_ref, half_ref, sems):
    width = half_ref.shape[2]
    parts = sems.shape[0]
    count = half_ref.shape[0] // parts
    columns = pl.ds(pl.multiple_of(side_ref[0] * width, width), width)
    copies = [
        pltpu.make_async_copy(
            grads_ref.at[pl.ds(i * count, count), :, columns],
            half_ref.at[pl.ds(i * count, count)],
            sems.at[i],
        )
        for i in range(parts)
    ]
    for copy in copies:
        copy.start()
    for copy in copies:
        copy.wait()


def column_half(side, grads):
    blocks, rows, width = grads.shape
    return pl.pallas_call(
        column_half_kernel,
        out_shape=jax.ShapeDtypeStruct((blocks, rows, width // 2), grads.dtype),
        in_specs=[SMEM, pl.BlockSpec(memory_space=pltpu.HBM)],
        out_specs=VMEM,
        scratch_shapes=[pltpu.SemaphoreType.DMA((COPIES,))],
        compiler_params=pltpu.CompilerParams(vmem_limit_bytes=32 * 2**20),
        name="column_half",
    )(side.reshape(1), grads)


def pair_sum_kernel(first, block_ref, own_ref, other_ref, out_ref):
    for p in range(out_ref.shape[0]):
        b = block_ref[first + p]
        out_ref[p] = own_ref[b] + other_ref[b]


def pair_sum(block_at, own, other, first, count):
    return pl.pallas_call(
        functools.partial(pair_sum_kernel, first),
        out_shape=jax.ShapeDtypeStruct((count,) + own.shape[1:], own.dtype),
        in_specs=[SMEM, VMEM, VMEM],
        out_specs=VMEM,
        compiler_params=pltpu.CompilerParams(vmem_limit_bytes=32 * 2**20),
        name="pair_sum",
    )(block_at, own, other)


def sum_to_owner_kernel(owner_ref, parts_ref, out_ref):
    out_ref[...] = jnp.zeros_like(out_ref)
    for j in range(parts_ref.shape[1]):
        total = parts_ref[0, j].astype(jnp.float32)
        for i in range(1, parts_ref.shape[0]):
            total = total + parts_ref[i, j].astype(jnp.float32)
        out_ref[owner_ref[j]] = total.astype(out_ref.dtype)


def sum_to_owner(owner, parts, owner_count):
    return pl.pallas_call(
        sum_to_owner_kernel,
        out_shape=jax.ShapeDtypeStruct((owner_count,) + parts.shape[2:], parts.dtype),
        in_specs=[SMEM, VMEM],
        out_specs=VMEM,
        compiler_params=pltpu.CompilerParams(vmem_limit_bytes=32 * 2**20),
        name="sum_to_owner",
    )(owner, parts)


def fetch_roots_kernel(
    slot_ref, core_ref, left_table, right_table, left_ref, right_ref, raw_ref, sems, *, slice_cols
):
    slot = slot_ref[0]
    left_copy = pltpu.make_async_copy(left_table.at[slot], left_ref, sems.at[0])
    right_copy = pltpu.make_async_copy(right_table.at[slot], raw_ref, sems.at[1])
    right_copy.start()
    left_copy.start()
    size = raw_ref.shape[0]
    half = size // 2
    column = lax.broadcasted_iota(jnp.int32, (size, size), 1)
    inner = column % half
    side = jnp.where(column < half, core_ref[0], 1 - core_ref[0])
    source = inner // slice_cols * (2 * slice_cols) + side * slice_cols + inner % slice_cols
    pick = (lax.broadcasted_iota(jnp.int32, (size, size), 0) == source).astype(jnp.bfloat16)
    right_copy.wait()
    ordered = jnp.dot(raw_ref[...], pick, preferred_element_type=jnp.float32)
    right_ref[...] = ordered.astype(right_ref.dtype)
    left_copy.wait()


def fetch_roots(slot, core, left_roots, right_roots, slice_cols):
    root = jax.ShapeDtypeStruct(left_roots.shape[1:], left_roots.dtype)
    hbm = pl.BlockSpec(memory_space=pltpu.HBM)
    return pl.pallas_call(
        functools.partial(fetch_roots_kernel, slice_cols=slice_cols),
        out_shape=(root, root),
        in_specs=[SMEM, SMEM, hbm, hbm],
        out_specs=(VMEM, VMEM),
        scratch_shapes=[
            pltpu.VMEM(root.shape, root.dtype),
            pltpu.SemaphoreType.DMA((2,)),
        ],
        compiler_params=pltpu.CompilerParams(vmem_limit_bytes=32 * 2**20),
        name="fetch_roots",
    )(
        slot.reshape(1),
        core.reshape(1),
        pltpu.with_memory_space_constraint(left_roots, pltpu.HBM),
        pltpu.with_memory_space_constraint(right_roots, pltpu.HBM),
    )


def half_product(core_ref, grad_ref, right_ref, opposite):
    size, half = right_ref.shape[0], grad_ref.shape[-1]
    side = 1 - core_ref[0] if opposite else core_ref[0]
    grad = grad_ref[...].reshape(size, half)
    factor = right_ref[pl.ds(pl.multiple_of(side * half, half), half), :]
    product = jnp.dot(grad, factor, preferred_element_type=jnp.float32)
    grad_float = grad.astype(jnp.float32)
    return product, jnp.sum(grad_float * grad_float, keepdims=True)


def own_product_kernel(core_ref, own_ref, right_ref, product_ref, squares_ref):
    product, squares = half_product(core_ref, own_ref, right_ref, False)
    product_ref[...] = product
    squares_ref[...] = jnp.broadcast_to(squares, squares_ref.shape)


def own_product(core, own, right_root):
    return pl.pallas_call(
        own_product_kernel,
        out_shape=(
            jax.ShapeDtypeStruct(right_root.shape, jnp.float32),
            jax.ShapeDtypeStruct((1, LANES), jnp.float32),
        ),
        in_specs=[SMEM, VMEM, VMEM],
        out_specs=(VMEM, VMEM),
        compiler_params=pltpu.CompilerParams(vmem_limit_bytes=32 * 2**20),
        name="own_product",
    )(core.reshape(1), own, right_root)


def precondition_kernel(
    core_ref, product_ref, squares_ref, other_ref, left_ref, right_ref, out_ref
):
    size = left_ref.shape[-1]
    half = other_ref.shape[-1]
    area = float(size * size)
    product, squares = half_product(core_ref, other_ref, right_ref, True)
    right_prod = (product_ref[...] + product).astype(jnp.bfloat16)
    grad_squares = squares_ref[:, :1] + squares
    precond = jnp.dot(left_ref[...], right_prod, preferred_element_type=jnp.float32)
    precond_squares = jnp.sum(precond * precond, keepdims=True)
    scale = jnp.sqrt(grad_squares / area) / jnp.sqrt(precond_squares / area + 1e-06)
    grafted = (precond[:, :half] * scale).astype(out_ref.dtype)
    out_ref[...] = grafted.reshape(out_ref.shape)


def precondition(core, product, squares, other, left_root, right_root):
    return pl.pallas_call(
        precondition_kernel,
        out_shape=jax.ShapeDtypeStruct(other.shape, other.dtype),
        in_specs=[SMEM, VMEM, VMEM, VMEM, VMEM, VMEM],
        out_specs=VMEM,
        compiler_params=pltpu.CompilerParams(vmem_limit_bytes=32 * 2**20),
        name="precondition",
    )(core.reshape(1), product, squares, other, left_root, right_root)


def split_columns_kernel(owner_ref, rows_ref, out_ref):
    replicas, groups, rows, lanes = out_ref.shape
    width = rows_ref.shape[-1] // replicas
    per = lanes // width
    lane = lax.broadcasted_iota(jnp.int32, (rows, lanes), 1) // width
    for g in range(groups):
        blocks = [rows_ref[owner_ref[g * per + i]].astype(jnp.float32) for i in range(per)]
        for t in range(replicas // per):
            tiles = [block[:, t * lanes : (t + 1) * lanes] for block in blocks]
            for k in range(per):
                mixed = tiles[k]
                for i in range(per):
                    if i != k:
                        moved = pltpu.roll(tiles[i], ((i - k) % per) * width, 1)
                        mixed = jnp.where(lane == i, moved, mixed)
                out_ref[t * per + k, g] = mixed.astype(out_ref.dtype)


def split_columns(owner, rows, replicas):
    count = owner.shape[0]
    width = rows.shape[-1] // replicas
    per = LANES // width
    shape = (replicas, count // per, rows.shape[1], LANES)
    return pl.pallas_call(
        split_columns_kernel,
        out_shape=jax.ShapeDtypeStruct(shape, rows.dtype),
        in_specs=[SMEM, VMEM],
        out_specs=VMEM,
        compiler_params=pltpu.CompilerParams(vmem_limit_bytes=32 * 2**20),
        name="split_columns",
    )(owner, rows)


def update_kernel(place_ref, momentum_ref, pieces_ref, out_ref, rows_ref, new_ref, sems):
    replicas, groups, rows, lanes = pieces_ref.shape
    width, count = momentum_ref.shape[1:]
    per = lanes // width
    depth = replicas * groups
    rows_ref[...] = pieces_ref[...].astype(jnp.float32).reshape(depth * rows, lanes)
    place = place_ref[...]
    turn = place % per
    group = lax.broadcasted_iota(jnp.int32, (depth, count), 0)
    pick = (group == place // per).astype(jnp.bfloat16)
    copies = []
    for row in range(rows):
        flipped = rows_ref[pl.ds(row, depth, stride=rows), :].T.astype(jnp.bfloat16)
        spread = jnp.dot(flipped, pick, preferred_element_type=jnp.float32)
        value = jnp.zeros((width, count), jnp.float32)
        for i in range(per):
            value = jnp.where(turn == i, spread[i * width : (i + 1) * width], value)
        new_ref[row] = 0.9 * momentum_ref[row] + 0.1 * value
        copies.append(pltpu.make_async_copy(new_ref.at[row], out_ref.at[row], sems.at[row]))
        copies[-1].start()
    for copy in copies:
        copy.wait()


def update(place, momentum, pieces):
    replicas, groups, rows, lanes = pieces.shape
    shape = (momentum.shape[1], momentum.shape[2], momentum.shape[0])
    flipped = pl.pallas_call(
        update_kernel,
        out_shape=jax.ShapeDtypeStruct(shape, momentum.dtype),
        in_specs=[VMEM, VMEM, VMEM],
        out_specs=pl.BlockSpec(memory_space=pltpu.HBM),
        scratch_shapes=[
            pltpu.VMEM((replicas * groups * rows, lanes), jnp.float32),
            pltpu.VMEM(shape, momentum.dtype),
            pltpu.SemaphoreType.DMA((rows,)),
        ],
        compiler_params=pltpu.CompilerParams(vmem_limit_bytes=32 * 2**20),
        name="update",
    )(place.reshape(1, -1), jnp.transpose(momentum, (1, 2, 0)), pieces)
    return jnp.transpose(flipped, (2, 0, 1))


def neighbour(place):
    x, core = place // 2, place % 2
    step = 1 if (x + core) % 2 == 0 else -1
    return (x + step) % 8 * 2 + core


def on_device(partial_grads, block_owner, block_slot, left_roots, right_roots, momentum):
    along_x = ("xh", "xl")
    rep = along_x + ("core",)
    fsdp = ("y", "z")
    owner_count = lax.axis_size(fsdp)
    planes = lax.axis_size(along_x)
    pairs = lax.axis_size("xh")
    cores = lax.axis_size("core")
    most = left_roots.shape[0]
    blocks, rows, width = partial_grads.shape[1:]
    each = blocks // planes
    half = width // cores
    core = lax.axis_index("core")
    plane = lax.axis_index(along_x).astype(jnp.uint32)
    parity = lax.axis_index("xl").astype(jnp.uint32)
    me = lax.axis_index(fsdp)

    swap = [(i, 1 - i) for i in range(cores)]
    grads = pltpu.with_memory_space_constraint(partial_grads[0], pltpu.HBM)
    away = column_half(1 - core, grads)
    other = lax.ppermute(away, "core", swap)
    core_later, away = lax.optimization_barrier((core, away))
    own = column_half(core_later, grads)
    own, owner_later, slot_later = lax.optimization_barrier((own, block_owner, block_slot))

    entry = owner_later * most + slot_later
    rank = jnp.sum((entry[None, :] < entry[:, None]).astype(jnp.uint32), axis=1)
    block_plane = rank % planes
    turn = rank // planes
    spot = ((block_plane + parity) % 2 * pairs + block_plane // 2) * each + turn
    order = lax.iota(jnp.uint32, blocks)
    block_at = jnp.sum(jnp.where(spot[None, :] == order[:, None], order[None, :], 0), axis=1)
    block_at = block_at.astype(jnp.int32)
    away = pair_sum(block_at, own, other, blocks // 2, blocks // 2)

    away, rank, block_at = lax.optimization_barrier((away, rank, block_at))
    keep = pair_sum(block_at, own, other, 0, blocks // 2)
    met = lax.ppermute(away, rep, [(i, neighbour(i)) for i in range(planes * cores)])
    place = (rank % planes * each + rank // planes).astype(jnp.int32)
    turns = lax.broadcasted_iota(jnp.uint32, (each, blocks), 0)
    turn_is = rank[None] == turns * planes + plane
    my_owner = jnp.sum(jnp.where(turn_is, block_owner[None], 0), axis=1)
    mine = (rank % planes == plane) & (block_owner == me)
    my_slot = jnp.sum(jnp.where(mine, block_slot, 0))
    left_root, right_root = fetch_roots(my_slot, core, left_roots, right_roots, half // planes)
    met, keep, left_root, right_root, my_owner, place = lax.optimization_barrier(
        (met, keep, left_root, right_root, my_owner, place)
    )

    parts = lax.all_to_all(
        (keep + met).reshape(pairs, each, rows, half), "xh", split_axis=0, concat_axis=0, tiled=True
    )
    to_owner = sum_to_owner(my_owner, parts, owner_count)
    grad_half = lax.all_to_all(to_owner, fsdp, split_axis=0, concat_axis=0, tiled=True)
    other_half = lax.ppermute(grad_half, "core", swap)
    product, squares = own_product(core, grad_half, right_root)
    grafted = precondition(core, product, squares, other_half, left_root, right_root)
    back = lax.all_to_all(grafted, fsdp, split_axis=0, concat_axis=0, tiled=True)
    pieces = split_columns(my_owner, back, planes)
    pieces = lax.all_to_all(pieces, along_x, split_axis=0, concat_axis=0, tiled=True)
    return update(place, momentum, pieces)


def solution(mesh):
    devices = mesh.devices.reshape(4, 2, 2, 8, 8)
    split = Mesh(devices, ("xh", "xl", "core", "y", "z"))
    rep, fsdp = ("xh", "xl", "core"), ("y", "z")
    in_specs = (
        P(rep, None, fsdp, None),
        P(),
        P(),
        P(fsdp, None, None),
        P(fsdp, None, None),
        P(None, fsdp, rep),
    )
    out_specs = P(None, fsdp, rep)
    return jax.shard_map(
        on_device, mesh=split, in_specs=in_specs, out_specs=out_specs, check_vma=False
    )
```

```python
import functools

import jax
import jax.numpy as jnp
from jax import lax
from jax.experimental import pallas as pl
from jax.experimental.pallas import tpu as pltpu
from jax.sharding import Mesh, PartitionSpec as P

LANES = 128
COPIES = 4
VMEM = pl.BlockSpec(memory_space=pltpu.VMEM)
SMEM = pl.BlockSpec(memory_space=pltpu.SMEM)


def column_half_kernel(side_ref, grads_ref, half_ref, sems):
    width = half_ref.shape[2]
    parts = sems.shape[0]
    count = half_ref.shape[0] // parts
    columns = pl.ds(pl.multiple_of(side_ref[0] * width, width), width)
    copies = [
        pltpu.make_async_copy(
            grads_ref.at[pl.ds(i * count, count), :, columns],
            half_ref.at[pl.ds(i * count, count)],
            sems.at[i],
        )
        for i in range(parts)
    ]
    for copy in copies:
        copy.start()
    for copy in copies:
        copy.wait()


def column_half(side, grads):
    blocks, rows, width = grads.shape
    return pl.pallas_call(
        column_half_kernel,
        out_shape=jax.ShapeDtypeStruct((blocks, rows, width // 2), grads.dtype),
        in_specs=[SMEM, pl.BlockSpec(memory_space=pltpu.HBM)],
        out_specs=VMEM,
        scratch_shapes=[pltpu.SemaphoreType.DMA((COPIES,))],
        compiler_params=pltpu.CompilerParams(vmem_limit_bytes=32 * 2**20),
        name="column_half",
    )(side.reshape(1), grads)


def pair_sum_kernel(first, block_ref, own_ref, other_ref, out_ref):
    for p in range(out_ref.shape[0]):
        b = block_ref[first + p]
        out_ref[p] = own_ref[b] + other_ref[b]


def pair_sum(block_at, own, other, first, count):
    return pl.pallas_call(
        functools.partial(pair_sum_kernel, first),
        out_shape=jax.ShapeDtypeStruct((count,) + own.shape[1:], own.dtype),
        in_specs=[SMEM, VMEM, VMEM],
        out_specs=VMEM,
        compiler_params=pltpu.CompilerParams(vmem_limit_bytes=32 * 2**20),
        name="pair_sum",
    )(block_at, own, other)


def sum_to_owner_kernel(owner_ref, parts_ref, out_ref):
    out_ref[...] = jnp.zeros_like(out_ref)
    for j in range(parts_ref.shape[1]):
        total = parts_ref[0, j].astype(jnp.float32)
        for i in range(1, parts_ref.shape[0]):
            total = total + parts_ref[i, j].astype(jnp.float32)
        out_ref[owner_ref[j]] = total.astype(out_ref.dtype)


def sum_to_owner(owner, parts, owner_count):
    return pl.pallas_call(
        sum_to_owner_kernel,
        out_shape=jax.ShapeDtypeStruct((owner_count,) + parts.shape[2:], parts.dtype),
        in_specs=[SMEM, VMEM],
        out_specs=VMEM,
        compiler_params=pltpu.CompilerParams(vmem_limit_bytes=32 * 2**20),
        name="sum_to_owner",
    )(owner, parts)


def fetch_roots_kernel(
    slot_ref, core_ref, left_table, right_table, left_ref, right_ref, raw_ref, sems, *, slice_cols
):
    slot = slot_ref[0]
    left_copy = pltpu.make_async_copy(left_table.at[slot], left_ref, sems.at[0])
    right_copy = pltpu.make_async_copy(right_table.at[slot], raw_ref, sems.at[1])
    right_copy.start()
    left_copy.start()
    size = raw_ref.shape[0]
    half = size // 2
    column = lax.broadcasted_iota(jnp.int32, (size, size), 1)
    inner = column % half
    side = jnp.where(column < half, core_ref[0], 1 - core_ref[0])
    source = inner // slice_cols * (2 * slice_cols) + side * slice_cols + inner % slice_cols
    pick = (lax.broadcasted_iota(jnp.int32, (size, size), 0) == source).astype(jnp.bfloat16)
    right_copy.wait()
    ordered = jnp.dot(raw_ref[...], pick, preferred_element_type=jnp.float32)
    right_ref[...] = ordered.astype(right_ref.dtype)
    left_copy.wait()


def fetch_roots(slot, core, left_roots, right_roots, slice_cols):
    root = jax.ShapeDtypeStruct(left_roots.shape[1:], left_roots.dtype)
    hbm = pl.BlockSpec(memory_space=pltpu.HBM)
    return pl.pallas_call(
        functools.partial(fetch_roots_kernel, slice_cols=slice_cols),
        out_shape=(root, root),
        in_specs=[SMEM, SMEM, hbm, hbm],
        out_specs=(VMEM, VMEM),
        scratch_shapes=[
            pltpu.VMEM(root.shape, root.dtype),
            pltpu.SemaphoreType.DMA((2,)),
        ],
        compiler_params=pltpu.CompilerParams(vmem_limit_bytes=32 * 2**20),
        name="fetch_roots",
    )(
        slot.reshape(1),
        core.reshape(1),
        pltpu.with_memory_space_constraint(left_roots, pltpu.HBM),
        pltpu.with_memory_space_constraint(right_roots, pltpu.HBM),
    )


def half_product(core_ref, grad_ref, right_ref, opposite):
    size, half = right_ref.shape[0], grad_ref.shape[-1]
    side = 1 - core_ref[0] if opposite else core_ref[0]
    grad = grad_ref[...].reshape(size, half)
    factor = right_ref[pl.ds(pl.multiple_of(side * half, half), half), :]
    product = jnp.dot(grad, factor, preferred_element_type=jnp.float32)
    grad_float = grad.astype(jnp.float32)
    return product, jnp.sum(grad_float * grad_float, keepdims=True)


def own_product_kernel(core_ref, own_ref, right_ref, product_ref, squares_ref):
    product, squares = half_product(core_ref, own_ref, right_ref, False)
    product_ref[...] = product
    squares_ref[...] = jnp.broadcast_to(squares, squares_ref.shape)


def own_product(core, own, right_root):
    return pl.pallas_call(
        own_product_kernel,
        out_shape=(
            jax.ShapeDtypeStruct(right_root.shape, jnp.float32),
            jax.ShapeDtypeStruct((1, LANES), jnp.float32),
        ),
        in_specs=[SMEM, VMEM, VMEM],
        out_specs=(VMEM, VMEM),
        compiler_params=pltpu.CompilerParams(vmem_limit_bytes=32 * 2**20),
        name="own_product",
    )(core.reshape(1), own, right_root)


def precondition_kernel(
    core_ref, product_ref, squares_ref, other_ref, left_ref, right_ref, out_ref
):
    size = left_ref.shape[-1]
    half = other_ref.shape[-1]
    area = float(size * size)
    product, squares = half_product(core_ref, other_ref, right_ref, True)
    right_prod = (product_ref[...] + product).astype(jnp.bfloat16)
    grad_squares = squares_ref[:, :1] + squares
    precond = jnp.dot(left_ref[...], right_prod, preferred_element_type=jnp.float32)
    precond_squares = jnp.sum(precond * precond, keepdims=True)
    scale = jnp.sqrt(grad_squares / area) / jnp.sqrt(precond_squares / area + 1e-06)
    grafted = (precond[:, :half] * scale).astype(out_ref.dtype)
    out_ref[...] = grafted.reshape(out_ref.shape)


def precondition(core, product, squares, other, left_root, right_root):
    return pl.pallas_call(
        precondition_kernel,
        out_shape=jax.ShapeDtypeStruct(other.shape, other.dtype),
        in_specs=[SMEM, VMEM, VMEM, VMEM, VMEM, VMEM],
        out_specs=VMEM,
        compiler_params=pltpu.CompilerParams(vmem_limit_bytes=32 * 2**20),
        name="precondition",
    )(core.reshape(1), product, squares, other, left_root, right_root)


def split_columns_kernel(owner_ref, rows_ref, out_ref):
    replicas, groups, rows, lanes = out_ref.shape
    width = rows_ref.shape[-1] // replicas
    per = lanes // width
    lane = lax.broadcasted_iota(jnp.int32, (rows, lanes), 1) // width
    for g in range(groups):
        blocks = [rows_ref[owner_ref[g * per + i]].astype(jnp.float32) for i in range(per)]
        for t in range(replicas // per):
            tiles = [block[:, t * lanes : (t + 1) * lanes] for block in blocks]
            for k in range(per):
                mixed = tiles[k]
                for i in range(per):
                    if i != k:
                        moved = pltpu.roll(tiles[i], ((i - k) % per) * width, 1)
                        mixed = jnp.where(lane == i, moved, mixed)
                out_ref[t * per + k, g] = mixed.astype(out_ref.dtype)


def split_columns(owner, rows, replicas):
    count = owner.shape[0]
    width = rows.shape[-1] // replicas
    per = LANES // width
    shape = (replicas, count // per, rows.shape[1], LANES)
    return pl.pallas_call(
        split_columns_kernel,
        out_shape=jax.ShapeDtypeStruct(shape, rows.dtype),
        in_specs=[SMEM, VMEM],
        out_specs=VMEM,
        compiler_params=pltpu.CompilerParams(vmem_limit_bytes=32 * 2**20),
        name="split_columns",
    )(owner, rows)


def update_kernel(place_ref, momentum_ref, pieces_ref, out_ref, rows_ref, new_ref, sems):
    replicas, groups, rows, lanes = pieces_ref.shape
    width, count = momentum_ref.shape[1:]
    per = lanes // width
    depth = replicas * groups
    rows_ref[...] = pieces_ref[...].astype(jnp.float32).reshape(depth * rows, lanes)
    place = place_ref[...]
    turn = place % per
    group = lax.broadcasted_iota(jnp.int32, (depth, count), 0)
    pick = (group == place // per).astype(jnp.bfloat16)
    copies = []
    for row in range(rows):
        flipped = rows_ref[pl.ds(row, depth, stride=rows), :].T.astype(jnp.bfloat16)
        spread = jnp.dot(flipped, pick, preferred_element_type=jnp.float32)
        value = jnp.zeros((width, count), jnp.float32)
        for i in range(per):
            value = jnp.where(turn == i, spread[i * width : (i + 1) * width], value)
        new_ref[row] = 0.9 * momentum_ref[row] + 0.1 * value
        copies.append(pltpu.make_async_copy(new_ref.at[row], out_ref.at[row], sems.at[row]))
        copies[-1].start()
    for copy in copies:
        copy.wait()


def update(place, momentum, pieces):
    replicas, groups, rows, lanes = pieces.shape
    shape = (momentum.shape[1], momentum.shape[2], momentum.shape[0])
    flipped = pl.pallas_call(
        update_kernel,
        out_shape=jax.ShapeDtypeStruct(shape, momentum.dtype),
        in_specs=[VMEM, VMEM, VMEM],
        out_specs=pl.BlockSpec(memory_space=pltpu.HBM),
        scratch_shapes=[
            pltpu.VMEM((replicas * groups * rows, lanes), jnp.float32),
            pltpu.VMEM(shape, momentum.dtype),
            pltpu.SemaphoreType.DMA((rows,)),
        ],
        compiler_params=pltpu.CompilerParams(vmem_limit_bytes=32 * 2**20),
        name="update",
    )(place.reshape(1, -1), jnp.transpose(momentum, (1, 2, 0)), pieces)
    return jnp.transpose(flipped, (2, 0, 1))


def partner(stage, x, core):
    y = (x - core) % 8
    y = (y ^ 1, y ^ 2, 7 - y)[stage]
    return (y + core) % 8


def partners(stage):
    return [(x * 2 + c, partner(stage, x, c) * 2 + c) for x in range(8) for c in range(2)]


def plane_orders():
    table = []
    for x in range(8):
        for core in range(2):
            planes = [x]
            for stage in (2, 1, 0):
                planes = planes + [partner(stage, p, core) for p in planes]
            table.append(planes)
    return table


def on_device(partial_grads, block_owner, block_slot, left_roots, right_roots, momentum):
    along_x = ("xh", "xl")
    rep = along_x + ("core",)
    fsdp = ("y", "z")
    owner_count = lax.axis_size(fsdp)
    planes = lax.axis_size(along_x)
    cores = lax.axis_size("core")
    most = left_roots.shape[0]
    blocks, rows, width = partial_grads.shape[1:]
    each = blocks // planes
    half = width // cores
    core = lax.axis_index("core")
    plane = lax.axis_index(along_x).astype(jnp.uint32)
    me = lax.axis_index(fsdp)

    swap = [(i, 1 - i) for i in range(cores)]
    grads = pltpu.with_memory_space_constraint(partial_grads[0], pltpu.HBM)
    away = column_half(1 - core, grads)
    other = lax.ppermute(away, "core", swap)
    core_later, away = lax.optimization_barrier((core, away))
    own = column_half(core_later, grads)
    own, owner_later, slot_later = lax.optimization_barrier((own, block_owner, block_slot))

    entry = owner_later * most + slot_later
    rank = jnp.sum((entry[None, :] < entry[:, None]).astype(jnp.uint32), axis=1)
    block_plane = rank % planes
    turn = rank // planes
    own_order = jnp.asarray(plane_orders(), jnp.uint32)[lax.axis_index(rep)]
    step = lax.iota(jnp.uint32, planes)
    at = jnp.sum(jnp.where(own_order[None, :] == block_plane[:, None], step[None, :], 0), axis=1)
    spot = at * each + turn
    order = lax.iota(jnp.uint32, blocks)
    block_at = jnp.sum(jnp.where(spot[None, :] == order[:, None], order[None, :], 0), axis=1)
    block_at = block_at.astype(jnp.int32)
    away = pair_sum(block_at, own, other, blocks // 2, blocks // 2)

    away, rank, block_at = lax.optimization_barrier((away, rank, block_at))
    keep = pair_sum(block_at, own, other, 0, blocks // 2)
    met = lax.ppermute(away, rep, partners(0))
    place = (rank % planes * each + rank // planes).astype(jnp.int32)
    turns = lax.broadcasted_iota(jnp.uint32, (each, blocks), 0)
    turn_is = rank[None] == turns * planes + plane
    my_owner = jnp.sum(jnp.where(turn_is, block_owner[None], 0), axis=1)
    mine = (rank % planes == plane) & (block_owner == me)
    my_slot = jnp.sum(jnp.where(mine, block_slot, 0))
    left_root, right_root = fetch_roots(my_slot, core, left_roots, right_roots, half // planes)
    met, keep, left_root, right_root, my_owner, place = lax.optimization_barrier(
        (met, keep, left_root, right_root, my_owner, place)
    )

    quarter, eighth = blocks // 4, blocks // 8
    away = keep[quarter:] + met[quarter:]
    met_next = lax.ppermute(away, rep, partners(1))
    keep = keep[:quarter] + met[:quarter]
    away = keep[eighth:] + met_next[eighth:]
    met_last = lax.ppermute(away, rep, partners(2))
    keep = keep[:eighth] + met_next[:eighth]
    parts = jnp.stack([keep, met_last])
    to_owner = sum_to_owner(my_owner, parts, owner_count)
    grad_half = lax.all_to_all(to_owner, fsdp, split_axis=0, concat_axis=0, tiled=True)
    other_half = lax.ppermute(grad_half, "core", swap)
    product, squares = own_product(core, grad_half, right_root)
    grafted = precondition(core, product, squares, other_half, left_root, right_root)
    back = lax.all_to_all(grafted, fsdp, split_axis=0, concat_axis=0, tiled=True)
    pieces = split_columns(my_owner, back, planes)
    pieces = lax.all_to_all(pieces, along_x, split_axis=0, concat_axis=0, tiled=True)
    return update(place, momentum, pieces)


def solution(mesh):
    devices = mesh.devices.reshape(4, 2, 2, 8, 8)
    split = Mesh(devices, ("xh", "xl", "core", "y", "z"))
    rep, fsdp = ("xh", "xl", "core"), ("y", "z")
    in_specs = (
        P(rep, None, fsdp, None),
        P(),
        P(),
        P(fsdp, None, None),
        P(fsdp, None, None),
        P(None, fsdp, rep),
    )
    out_specs = P(None, fsdp, rep)
    return jax.shard_map(
        on_device, mesh=split, in_specs=in_specs, out_specs=out_specs, check_vma=False
    )
```

```python
import functools

import jax
import jax.numpy as jnp
from jax import lax
from jax.experimental import pallas as pl
from jax.experimental.pallas import tpu as pltpu
from jax.sharding import Mesh, PartitionSpec as P

LANES = 128
COPIES = 4
VMEM = pl.BlockSpec(memory_space=pltpu.VMEM)
SMEM = pl.BlockSpec(memory_space=pltpu.SMEM)


def column_half_kernel(side_ref, grads_ref, half_ref, sems):
    width = half_ref.shape[2]
    parts = sems.shape[0]
    count = half_ref.shape[0] // parts
    columns = pl.ds(pl.multiple_of(side_ref[0] * width, width), width)
    copies = [
        pltpu.make_async_copy(
            grads_ref.at[pl.ds(i * count, count), :, columns],
            half_ref.at[pl.ds(i * count, count)],
            sems.at[i],
        )
        for i in range(parts)
    ]
    for copy in copies:
        copy.start()
    for copy in copies:
        copy.wait()


def column_half(side, grads):
    blocks, rows, width = grads.shape
    return pl.pallas_call(
        column_half_kernel,
        out_shape=jax.ShapeDtypeStruct((blocks, rows, width // 2), grads.dtype),
        in_specs=[SMEM, pl.BlockSpec(memory_space=pltpu.HBM)],
        out_specs=VMEM,
        scratch_shapes=[pltpu.SemaphoreType.DMA((COPIES,))],
        compiler_params=pltpu.CompilerParams(vmem_limit_bytes=32 * 2**20),
        name="column_half",
    )(side.reshape(1), grads)


def pair_sum_kernel(first, block_ref, own_ref, other_ref, out_ref):
    for p in range(out_ref.shape[0]):
        b = block_ref[first + p]
        out_ref[p] = own_ref[b] + other_ref[b]


def pair_sum(block_at, own, other, first, count):
    return pl.pallas_call(
        functools.partial(pair_sum_kernel, first),
        out_shape=jax.ShapeDtypeStruct((count,) + own.shape[1:], own.dtype),
        in_specs=[SMEM, VMEM, VMEM],
        out_specs=VMEM,
        compiler_params=pltpu.CompilerParams(vmem_limit_bytes=32 * 2**20),
        name="pair_sum",
    )(block_at, own, other)


def sum_to_owner_kernel(owner_ref, parts_ref, out_ref):
    out_ref[...] = jnp.zeros_like(out_ref)
    for j in range(parts_ref.shape[1]):
        total = parts_ref[0, j].astype(jnp.float32)
        for i in range(1, parts_ref.shape[0]):
            total = total + parts_ref[i, j].astype(jnp.float32)
        out_ref[owner_ref[j]] = total.astype(out_ref.dtype)


def sum_to_owner(owner, parts, owner_count):
    return pl.pallas_call(
        sum_to_owner_kernel,
        out_shape=jax.ShapeDtypeStruct((owner_count,) + parts.shape[2:], parts.dtype),
        in_specs=[SMEM, VMEM],
        out_specs=VMEM,
        compiler_params=pltpu.CompilerParams(vmem_limit_bytes=32 * 2**20),
        name="sum_to_owner",
    )(owner, parts)


def fetch_roots_kernel(
    slot_ref, core_ref, left_table, right_table, left_ref, right_ref, raw_ref, sems, *, slice_cols
):
    slot = slot_ref[0]
    left_copy = pltpu.make_async_copy(left_table.at[slot], left_ref, sems.at[0])
    right_copy = pltpu.make_async_copy(right_table.at[slot], raw_ref, sems.at[1])
    right_copy.start()
    left_copy.start()
    size = raw_ref.shape[0]
    half = size // 2
    column = lax.broadcasted_iota(jnp.int32, (size, size), 1)
    inner = column % half
    side = jnp.where(column < half, core_ref[0], 1 - core_ref[0])
    source = inner // slice_cols * (2 * slice_cols) + side * slice_cols + inner % slice_cols
    pick = (lax.broadcasted_iota(jnp.int32, (size, size), 0) == source).astype(jnp.bfloat16)
    right_copy.wait()
    ordered = jnp.dot(raw_ref[...], pick, preferred_element_type=jnp.float32)
    right_ref[...] = ordered.astype(right_ref.dtype)
    left_copy.wait()


def fetch_roots(slot, core, left_roots, right_roots, slice_cols):
    root = jax.ShapeDtypeStruct(left_roots.shape[1:], left_roots.dtype)
    hbm = pl.BlockSpec(memory_space=pltpu.HBM)
    return pl.pallas_call(
        functools.partial(fetch_roots_kernel, slice_cols=slice_cols),
        out_shape=(root, root),
        in_specs=[SMEM, SMEM, hbm, hbm],
        out_specs=(VMEM, VMEM),
        scratch_shapes=[
            pltpu.VMEM(root.shape, root.dtype),
            pltpu.SemaphoreType.DMA((2,)),
        ],
        compiler_params=pltpu.CompilerParams(vmem_limit_bytes=32 * 2**20),
        name="fetch_roots",
    )(
        slot.reshape(1),
        core.reshape(1),
        pltpu.with_memory_space_constraint(left_roots, pltpu.HBM),
        pltpu.with_memory_space_constraint(right_roots, pltpu.HBM),
    )


def half_product(core_ref, grad_ref, right_ref, opposite):
    size, half = right_ref.shape[0], grad_ref.shape[-1]
    side = 1 - core_ref[0] if opposite else core_ref[0]
    grad = grad_ref[...].reshape(size, half)
    factor = right_ref[pl.ds(pl.multiple_of(side * half, half), half), :]
    product = jnp.dot(grad, factor, preferred_element_type=jnp.float32)
    grad_float = grad.astype(jnp.float32)
    return product, jnp.sum(grad_float * grad_float, keepdims=True)


def own_product_kernel(core_ref, own_ref, right_ref, product_ref, squares_ref):
    product, squares = half_product(core_ref, own_ref, right_ref, False)
    product_ref[...] = product
    squares_ref[...] = jnp.broadcast_to(squares, squares_ref.shape)


def own_product(core, own, right_root):
    return pl.pallas_call(
        own_product_kernel,
        out_shape=(
            jax.ShapeDtypeStruct(right_root.shape, jnp.float32),
            jax.ShapeDtypeStruct((1, LANES), jnp.float32),
        ),
        in_specs=[SMEM, VMEM, VMEM],
        out_specs=(VMEM, VMEM),
        compiler_params=pltpu.CompilerParams(vmem_limit_bytes=32 * 2**20),
        name="own_product",
    )(core.reshape(1), own, right_root)


def precondition_kernel(
    core_ref, product_ref, squares_ref, other_ref, left_ref, right_ref, out_ref
):
    size = left_ref.shape[-1]
    half = other_ref.shape[-1]
    area = float(size * size)
    product, squares = half_product(core_ref, other_ref, right_ref, True)
    right_prod = (product_ref[...] + product).astype(jnp.bfloat16)
    grad_squares = squares_ref[:, :1] + squares
    count = 128
    precond_squares = jnp.zeros((1, 1), jnp.float32)
    kept = []
    for start in range(0, size, count):
        precond = jnp.dot(
            left_ref[start : start + count, :], right_prod, preferred_element_type=jnp.float32
        )
        precond_squares += jnp.sum(precond * precond, keepdims=True)
        kept.append(precond[:, :half])
    scale = jnp.sqrt(grad_squares / area) / jnp.sqrt(precond_squares / area + 1e-06)
    rows = out_ref.shape[1]
    for i, part in enumerate(kept):
        grafted = (part * scale).astype(out_ref.dtype)
        out_ref[i * count // rows : (i + 1) * count // rows] = grafted.reshape(-1, rows, half)


def precondition(core, product, squares, other, left_root, right_root):
    return pl.pallas_call(
        precondition_kernel,
        out_shape=jax.ShapeDtypeStruct(other.shape, other.dtype),
        in_specs=[SMEM, VMEM, VMEM, VMEM, VMEM, VMEM],
        out_specs=VMEM,
        compiler_params=pltpu.CompilerParams(vmem_limit_bytes=32 * 2**20),
        name="precondition",
    )(core.reshape(1), product, squares, other, left_root, right_root)


def split_columns_kernel(owner_ref, rows_ref, out_ref):
    replicas, groups, rows, lanes = out_ref.shape
    width = rows_ref.shape[-1] // replicas
    per = lanes // width
    lane = lax.broadcasted_iota(jnp.int32, (rows, lanes), 1) // width
    for g in range(groups):
        blocks = [rows_ref[owner_ref[g * per + i]].astype(jnp.float32) for i in range(per)]
        for t in range(replicas // per):
            tiles = [block[:, t * lanes : (t + 1) * lanes] for block in blocks]
            for k in range(per):
                mixed = tiles[k]
                for i in range(per):
                    if i != k:
                        moved = pltpu.roll(tiles[i], ((i - k) % per) * width, 1)
                        mixed = jnp.where(lane == i, moved, mixed)
                out_ref[t * per + k, g] = mixed.astype(out_ref.dtype)


def split_columns(owner, rows, replicas):
    count = owner.shape[0]
    width = rows.shape[-1] // replicas
    per = LANES // width
    shape = (replicas, count // per, rows.shape[1], LANES)
    return pl.pallas_call(
        split_columns_kernel,
        out_shape=jax.ShapeDtypeStruct(shape, rows.dtype),
        in_specs=[SMEM, VMEM],
        out_specs=VMEM,
        compiler_params=pltpu.CompilerParams(vmem_limit_bytes=32 * 2**20),
        name="split_columns",
    )(owner, rows)


def update_kernel(place_ref, momentum_ref, pieces_ref, out_ref, rows_ref, new_ref, sems):
    replicas, groups, rows, lanes = pieces_ref.shape
    width, count = momentum_ref.shape[1:]
    per = lanes // width
    depth = replicas * groups
    rows_ref[...] = pieces_ref[...].astype(jnp.float32).reshape(depth * rows, lanes)
    place = place_ref[...]
    turn = place % per
    group = lax.broadcasted_iota(jnp.int32, (depth, count), 0)
    pick = (group == place // per).astype(jnp.bfloat16)
    copies = []
    for row in range(rows):
        flipped = rows_ref[pl.ds(row, depth, stride=rows), :].T.astype(jnp.bfloat16)
        spread = jnp.dot(flipped, pick, preferred_element_type=jnp.float32)
        value = jnp.zeros((width, count), jnp.float32)
        for i in range(per):
            value = jnp.where(turn == i, spread[i * width : (i + 1) * width], value)
        new_ref[row] = 0.9 * momentum_ref[row] + 0.1 * value
        copies.append(pltpu.make_async_copy(new_ref.at[row], out_ref.at[row], sems.at[row]))
        copies[-1].start()
    for copy in copies:
        copy.wait()


def update(place, momentum, pieces):
    replicas, groups, rows, lanes = pieces.shape
    shape = (momentum.shape[1], momentum.shape[2], momentum.shape[0])
    flipped = pl.pallas_call(
        update_kernel,
        out_shape=jax.ShapeDtypeStruct(shape, momentum.dtype),
        in_specs=[VMEM, VMEM, VMEM],
        out_specs=pl.BlockSpec(memory_space=pltpu.HBM),
        scratch_shapes=[
            pltpu.VMEM((replicas * groups * rows, lanes), jnp.float32),
            pltpu.VMEM(shape, momentum.dtype),
            pltpu.SemaphoreType.DMA((rows,)),
        ],
        compiler_params=pltpu.CompilerParams(vmem_limit_bytes=32 * 2**20),
        name="update",
    )(place.reshape(1, -1), jnp.transpose(momentum, (1, 2, 0)), pieces)
    return jnp.transpose(flipped, (2, 0, 1))


def neighbour(place):
    x, core = place // 2, place % 2
    step = 1 if (x + core) % 2 == 0 else -1
    return (x + step) % 8 * 2 + core


def on_device(partial_grads, block_owner, block_slot, left_roots, right_roots, momentum):
    along_x = ("xh", "xl")
    rep = along_x + ("core",)
    fsdp = ("y", "z")
    owner_count = lax.axis_size(fsdp)
    planes = lax.axis_size(along_x)
    pairs = lax.axis_size("xh")
    cores = lax.axis_size("core")
    most = left_roots.shape[0]
    blocks, rows, width = partial_grads.shape[1:]
    each = blocks // planes
    half = width // cores
    core = lax.axis_index("core")
    plane = lax.axis_index(along_x).astype(jnp.uint32)
    parity = lax.axis_index("xl").astype(jnp.uint32)
    me = lax.axis_index(fsdp)

    swap = [(i, 1 - i) for i in range(cores)]
    grads = pltpu.with_memory_space_constraint(partial_grads[0], pltpu.HBM)
    away = column_half(1 - core, grads)
    other = lax.ppermute(away, "core", swap)
    core_later, away = lax.optimization_barrier((core, away))
    own = column_half(core_later, grads)
    own, owner_later, slot_later = lax.optimization_barrier((own, block_owner, block_slot))

    entry = owner_later * most + slot_later
    rank = jnp.sum((entry[None, :] < entry[:, None]).astype(jnp.uint32), axis=1)
    block_plane = rank % planes
    turn = rank // planes
    spot = ((block_plane + parity) % 2 * pairs + block_plane // 2) * each + turn
    order = lax.iota(jnp.uint32, blocks)
    block_at = jnp.sum(jnp.where(spot[None, :] == order[:, None], order[None, :], 0), axis=1)
    block_at = block_at.astype(jnp.int32)
    away = pair_sum(block_at, own, other, blocks // 2, blocks // 2)

    away, rank, block_at = lax.optimization_barrier((away, rank, block_at))
    keep = pair_sum(block_at, own, other, 0, blocks // 2)
    met = lax.ppermute(away, rep, [(i, neighbour(i)) for i in range(planes * cores)])
    place = (rank % planes * each + rank // planes).astype(jnp.int32)
    turns = lax.broadcasted_iota(jnp.uint32, (each, blocks), 0)
    turn_is = rank[None] == turns * planes + plane
    my_owner = jnp.sum(jnp.where(turn_is, block_owner[None], 0), axis=1)
    mine = (rank % planes == plane) & (block_owner == me)
    my_slot = jnp.sum(jnp.where(mine, block_slot, 0))
    left_root, right_root = fetch_roots(my_slot, core, left_roots, right_roots, half // planes)
    met, keep, left_root, right_root, my_owner, place = lax.optimization_barrier(
        (met, keep, left_root, right_root, my_owner, place)
    )

    parts = lax.all_to_all(
        (keep + met).reshape(pairs, each, rows, half), "xh", split_axis=0, concat_axis=0, tiled=True
    )
    to_owner = sum_to_owner(my_owner, parts, owner_count)
    grad_half = lax.all_to_all(to_owner, fsdp, split_axis=0, concat_axis=0, tiled=True)
    other_half = lax.ppermute(grad_half, "core", swap)
    product, squares = own_product(core, grad_half, right_root)
    grafted = precondition(core, product, squares, other_half, left_root, right_root)
    back = lax.all_to_all(grafted, fsdp, split_axis=0, concat_axis=0, tiled=True)
    pieces = split_columns(my_owner, back, planes)
    pieces = lax.all_to_all(pieces, along_x, split_axis=0, concat_axis=0, tiled=True)
    return update(place, momentum, pieces)


def solution(mesh):
    devices = mesh.devices.reshape(4, 2, 2, 8, 8)
    split = Mesh(devices, ("xh", "xl", "core", "y", "z"))
    rep, fsdp = ("xh", "xl", "core"), ("y", "z")
    in_specs = (
        P(rep, None, fsdp, None),
        P(),
        P(),
        P(fsdp, None, None),
        P(fsdp, None, None),
        P(None, fsdp, rep),
    )
    out_specs = P(None, fsdp, rep)
    return jax.shard_map(
        on_device, mesh=split, in_specs=in_specs, out_specs=out_specs, check_vma=False
    )
```
